512 devices in a mesh: enc: 64 (over x, y, core), tp: 8 (over z).
Axes of the slice: x: 4, y: 8, z: 8, core: 2. Of those that a mesh axis runs over, the one named last changes fastest.
Arguments:
- queries: bfloat16 [8192, 4096], P('enc', 'tp'), may hold values from -3 to 3
- out_grad: bfloat16 [8192, 4096], P('enc', 'tp'), may hold values from -8 to 8
- encodings: bfloat16 [64, 128, 896], P('enc', 'tp'), may hold values from -3 to 3
- kv_weight: bfloat16 [2, 896, 4096], P(None, None, 'tp'), may hold values from -0.1875 to 0.1875
- neighbour_ids: int32 [128, 2], P('enc'), may hold values from 0 to 63
- rot_offset: int32 [128, 2], P('enc'), may hold values from 0 to 255
Outputs:
- grad_query: bfloat16 [8192, 4096], P('enc', 'tp')
- grad_encodings: float32 [64, 128, 896], P('enc', 'tp')
The draws below stay inside these ranges and needn't reach their ends.
Inputs may be any that keep to these rules, and one draw needn't show every extreme that they name: `neighbour_ids`: block index = owner index of enc times 1 plus the owner's own block.
All inputs are finite; a program needn't handle non-finite values.
Results may differ from the reference program's by a relative error of at most 0.011.
Values may be sent and summed in bfloat16 or wider, within the bound.
No kernel may reach another device: no remote copies, remote signals or barrier semaphores. Data moves between devices by JAX's collectives and lax.ppermute only.
A program may use at most 64 MiB of HBM per device.

```python
import math
import jax
import jax.numpy as jnp
import numpy as np
from jax import lax

HEADS = 32
HEAD = 128
DE = 896
SPAN = 64
NEIGH = 2
NLEN = 128
SPANS = 128
TOKENS = 8192
BLOCKS = 64


def with_ends(entries, own_key, low, high):
    spot = [jax.random.randint(jax.random.fold_in(own_key, axis), (), 0, length) for axis, length in enumerate(entries.shape)]
    longest = entries.shape.index(max(entries.shape))
    beside = spot[:longest] + [(spot[longest] + 1) % entries.shape[longest]] + spot[longest + 1:]
    return entries.at[tuple(spot)].set(low).at[tuple(beside)].set(high)


def steps_of(stream_key, extent, pieces, least, largest):
    level, own = 1.0, jax.random.fold_in(stream_key, 6)
    for axis_at, shards_of in pieces:
        steps = jnp.exp(jax.random.uniform(jax.random.fold_in(own, axis_at), (shards_of,), jnp.float32, least / len(pieces), largest / len(pieces)))
        level = level * jnp.repeat(steps, extent[axis_at] // shards_of).reshape([-1 if axis == axis_at else 1 for axis in range(len(extent))])
    return level


def rank_bounds(number_of, slope):
    weights = [(1 << 20) // math.isqrt(grade ** slope) + 1 for grade in range(1, number_of + 1)]
    deviation = 1 + sum(weights) // (1 << 30)
    return np.cumsum(np.array([max(1, weight // deviation) for weight in weights]))


def ranked_ids(own_key, dims, amount, lean):
    table = rank_bounds(amount, lean)
    pick = jax.random.randint(jax.random.fold_in(own_key, 1), dims, 0, int(table[amount - 1]))
    grade = jnp.searchsorted(jnp.asarray(table, jnp.int32), pick, side="right")
    return jax.random.permutation(jax.random.fold_in(own_key, 2), amount)[grade].astype(jnp.int32)


def bell_draw(rng, extent, spread, bound, pieces=(), kind=jnp.bfloat16):
    array = spread * jax.random.normal(rng, extent, jnp.float32)
    if pieces:
        array = array * steps_of(rng, extent, pieces, -0.22, 0.18)
    return jnp.clip(array, -bound, bound).astype(kind)


def setup_inputs(seed: int = 0) -> dict:
    streams_of = jax.random.split(jax.random.key(seed), 7)
    return {
        "queries": bell_draw(streams_of[0], (TOKENS, HEADS * HEAD), 1.0, 3.0, ((0, 64), (1, 8))),
        "out_grad": bell_draw(streams_of[1], (TOKENS, HEADS * HEAD), 2.0, 8.0, ((0, 64), (1, 8))),
        "encodings": bell_draw(streams_of[2], (BLOCKS, NLEN, DE), 1.0, 3.0, ((0, 64), (1, 8))),
        "kv_weight": bell_draw(streams_of[3], (2, DE, HEADS * HEAD), DE ** -0.5, 0.1875, ((2, 8),)),
        "neighbour_ids": with_ends(ranked_ids(streams_of[4], (SPANS, NEIGH), BLOCKS, 2), jax.random.fold_in(streams_of[4], 3), 0, BLOCKS - 1).astype(jnp.int32),
        "rot_offset": with_ends(jax.random.randint(streams_of[5], (SPANS, NEIGH), 0, 4 * SPAN), jax.random.fold_in(streams_of[5], 1), 0, (4 * SPAN) - 1).astype(jnp.int32),
    }


def rotary_tables(positions, head_width):
    halfway = head_width // 2
    exponent = jnp.arange(halfway, dtype=jnp.float32) * (2.0 / head_width)
    frequency = jnp.exp(-math.log(10000.0) * exponent)
    angles = positions.astype(jnp.float32)[:, None] * frequency[None, :]
    return (jnp.cos(angles), jnp.sin(angles))

def rotate(vectors, cosine, sine_table):
    halfway = vectors.shape[-1] // 2
    former = vectors[..., :halfway]
    latter = vectors[..., halfway:]
    return jnp.concatenate([former * cosine - latter * sine_table, former * sine_table + latter * cosine], axis=-1)

def rotate_back(vectors, cosine, sine_table):
    halfway = vectors.shape[-1] // 2
    former = vectors[..., :halfway]
    latter = vectors[..., halfway:]
    return jnp.concatenate([former * cosine + latter * sine_table, latter * cosine - former * sine_table], axis=-1)

def widened(lowered):
    return lax.optimization_barrier(lowered).astype(jnp.float32)

def reference(queries, out_grad, encodings, kv_weight, neighbour_ids, rot_offset):
    full_width = HEADS * HEAD
    score_scale = 1.0 / math.sqrt(HEAD)
    flat_rows = encodings.reshape(BLOCKS * NLEN, DE)
    key_raw = jnp.dot(flat_rows, kv_weight[0], preferred_element_type=jnp.float32).reshape(BLOCKS, NLEN, HEADS, HEAD)
    values_all = jnp.dot(flat_rows, kv_weight[1], preferred_element_type=jnp.float32).astype(jnp.bfloat16).reshape(BLOCKS, NLEN, HEADS, HEAD)
    query_cos, query_sin = rotary_tables(jnp.arange(SPAN, dtype=jnp.int32), HEAD)
    query_cos = query_cos[:, None, :]
    query_sin = query_sin[:, None, :]

    def one_span(inputs):
        query_rows, grad_rows, block_ids, offsets = inputs
        query_rot = rotate(query_rows.astype(jnp.float32).reshape(SPAN, HEADS, HEAD), query_cos, query_sin).astype(jnp.bfloat16)
        key_parts = []
        value_parts = []
        tables = []
        for member in range(NEIGH):
            cosine, sine_table = rotary_tables(jnp.arange(NLEN, dtype=jnp.int32) + offsets[member], HEAD)
            cosine = cosine[:, None, :]
            sine_table = sine_table[:, None, :]
            tables.append((cosine, sine_table))
            key_parts.append(rotate(key_raw[block_ids[member]], cosine, sine_table).astype(jnp.bfloat16))
            value_parts.append(values_all[block_ids[member]])
        keys_wide = widened(jnp.concatenate(key_parts, axis=0))
        values_wide = widened(jnp.concatenate(value_parts, axis=0))
        query_wide = widened(query_rot)
        scores = jnp.einsum('qhd,khd->hqk', query_wide, keys_wide) * score_scale
        exponentials = jnp.exp(scores)
        weights = exponentials / lax.optimization_barrier(jnp.sum(exponentials, axis=-1, keepdims=True))
        weights_wide = widened(weights.astype(jnp.bfloat16))
        attended = jnp.einsum('hqk,khd->qhd', weights_wide, values_wide)
        grads = grad_rows.astype(jnp.float32).reshape(SPAN, HEADS, HEAD)
        row_dots = lax.optimization_barrier(jnp.sum(grads * attended, axis=-1))
        grad_values = jnp.einsum('hqk,qhd->khd', weights_wide, grads).astype(jnp.bfloat16)
        grad_weights = jnp.einsum('qhd,khd->hqk', grads, values_wide)
        grad_scores = (weights * (grad_weights - jnp.transpose(row_dots)[:, :, None]) * score_scale).astype(jnp.bfloat16)
        scores_wide = widened(grad_scores)
        grad_rot = jnp.einsum('hqk,khd->qhd', scores_wide, keys_wide)
        grad_query = rotate_back(grad_rot, query_cos, query_sin).astype(jnp.bfloat16).reshape(SPAN, full_width)
        grad_keys_rot = jnp.einsum('hqk,qhd->khd', scores_wide, query_wide)
        key_grads = []
        for member in range(NEIGH):
            cosine, sine_table = tables[member]
            part_rows = grad_keys_rot[member * NLEN:(member + 1) * NLEN]
            key_grads.append(rotate_back(part_rows, cosine, sine_table).astype(jnp.bfloat16))
        return (grad_query, jnp.stack(key_grads, axis=0), grad_values.reshape(NEIGH, NLEN, HEADS, HEAD))
    query_spans = queries.reshape(SPANS, SPAN, full_width)
    grad_spans = out_grad.reshape(SPANS, SPAN, full_width)
    grad_query, grad_keys, grad_values = lax.map(one_span, (query_spans, grad_spans, neighbour_ids, rot_offset))
    flat_ids = neighbour_ids.reshape(SPANS * NEIGH)
    key_sums = jnp.zeros((BLOCKS, NLEN, full_width), jnp.float32).at[flat_ids].add(grad_keys.reshape(SPANS * NEIGH, NLEN, full_width).astype(jnp.float32))
    value_sums = jnp.zeros((BLOCKS, NLEN, full_width), jnp.float32).at[flat_ids].add(grad_values.reshape(SPANS * NEIGH, NLEN, full_width).astype(jnp.float32))
    weight_key = kv_weight[0].astype(jnp.float32)
    weight_value = kv_weight[1].astype(jnp.float32)
    grad_enc = jnp.dot(key_sums.reshape(BLOCKS * NLEN, full_width), weight_key.T, precision=lax.Precision.HIGHEST)
    grad_enc = grad_enc + jnp.dot(value_sums.reshape(BLOCKS * NLEN, full_width), weight_value.T, precision=lax.Precision.HIGHEST)
    return (grad_query.reshape(TOKENS, full_width), grad_enc.reshape(BLOCKS, NLEN, DE))
```

```python
import math

import jax
import jax.numpy as jnp
from jax import lax
from jax.experimental import pallas as pl
from jax.experimental.pallas import tpu as pltpu
from jax.sharding import Mesh, PartitionSpec as P

HEAD = 128
DE = 896
SPAN = 64
NEIGH = 2
NLEN = 128
NX, NY, NC, NZ = 4, 8, 2, 8
ROWS = NLEN // NZ
F32, BF16 = jnp.float32, jnp.bfloat16
VMEM = pl.BlockSpec(memory_space=pltpu.VMEM)
SMEM = pl.BlockSpec(memory_space=pltpu.SMEM)


def rotary_tables(positions):
    halfway = HEAD // 2
    exponent = jnp.arange(halfway, dtype=F32) * (2.0 / HEAD)
    frequency = jnp.exp(-math.log(10000.0) * exponent)
    angles = positions.astype(F32)[:, None] * frequency[None, :]
    cosine, sine = jnp.cos(angles), jnp.sin(angles)
    return jnp.concatenate([cosine, cosine], axis=-1), jnp.concatenate([-sine, sine], axis=-1)


def shifted(value, axis, size, shift):
    return lax.ppermute(value, axis, [(i, (i + shift) % size) for i in range(size)])


def swapped(value, axis, size):
    return lax.ppermute(value, axis, [(i, i ^ 1) for i in range(size)])


def dot(a, b, over=(1, 0)):
    return lax.dot_general(
        a, b, (((over[0],), (over[1],)), ((), ())), preferred_element_type=F32
    )


def near_id(near_ref, column, read, reads):
    distance = lax.rem(near_ref[NX * reads] - column + NX, NX)
    return near_ref[distance * reads + read]


def pick_kernel(near_ref, mine_ref, theirs_ref, out_ref):
    core, reads = near_ref[near_ref.shape[0] - 1], out_ref.shape[1]
    for column in range(NX):
        for read in range(reads):
            block = near_id(near_ref, column, read, reads)
            row, same = lax.rem(block // NC, NY), lax.rem(block, NC) == core

            @pl.when(same)
            def _():
                out_ref[column, read] = mine_ref[row]

            @pl.when(jnp.logical_not(same))
            def _():
                out_ref[column, read] = theirs_ref[row]


def spread_kernel(near_ref, from_ref, out_ref):
    reads = from_ref.shape[1]
    spans = reads // NEIGH
    for read in range(reads):
        block = from_ref[near_ref[read] // (NY * NC), read]
        for at in range(read // NEIGH, NZ, spans):
            out_ref[at, read % NEIGH] = block


def owner_kernel(near_ref, from_ref, mine_ref, theirs_ref, total):
    total[...] = jnp.zeros_like(total)
    reads = from_ref.shape[1]
    here, core = near_ref[NX * reads], near_ref[near_ref.shape[0] - 1]
    for column in range(NX):
        for read in range(reads):
            block = near_id(near_ref, column, read, reads)

            @pl.when(block // (NY * NC) == here)
            def _():
                side = jnp.where(lax.rem(block, NC) == core, 0, NY)
                at = side + lax.rem(block // NC, NY)
                total[at] = total[at] + from_ref[column, read].astype(F32)

    mine_ref[...] = total[:NY]
    theirs_ref[...] = total[NY:].astype(BF16)


def attention_kernel(
    tok, w_own, w_pair, q_own, q_pair, g_own, g_pair, kc, ks, qc, qs,
    part, dq_own, dq_pair, dk_all, dv_all, total,
):
    scale = 1.0 / math.sqrt(HEAD)
    rows = jnp.concatenate([tok[:, n].reshape(NLEN, DE) for n in range(NEIGH)], axis=0)
    key_cos, key_sin, query_cos, query_sin = kc[...], ks[...], qc[...], qs[...]
    half = HEAD // 2
    for turn, (w, q, g, dq) in enumerate(
        ((w_own, q_own, g_own, dq_own), (w_pair, q_pair, g_pair, dq_pair))
    ):
        key_raw = dot(rows, w[0])
        values = dot(rows, w[1]).astype(BF16)
        for head in range(w.shape[2] // HEAD):
            cols = slice(head * HEAD, (head + 1) * HEAD)
            raw = key_raw[:, cols]
            key = (raw * key_cos + pltpu.roll(raw, half, 1) * key_sin).astype(BF16)
            value = values[:, cols]
            wide = q[:, cols].astype(F32)
            query = (wide * query_cos + pltpu.roll(wide, half, 1) * query_sin).astype(BF16)
            grad = g[:, cols]
            exponentials = jnp.exp(dot(query, key, (1, 1)) * scale)
            weights = exponentials / jnp.sum(exponentials, axis=-1, keepdims=True)
            weights_low = weights.astype(BF16)
            grad_weights = dot(grad, value, (1, 1))
            delta = jnp.sum(weights_low.astype(F32) * grad_weights, axis=-1, keepdims=True)
            grad_scores = (weights * (grad_weights - delta) * scale).astype(BF16)
            dv_all[:, cols] = dot(weights_low, grad, (0, 0)).astype(BF16)
            grad_query = dot(grad_scores, key)
            dq[:, cols] = (
                grad_query * query_cos - pltpu.roll(grad_query, half, 1) * query_sin
            ).astype(BF16)
            grad_key = dot(grad_scores, query, (0, 0))
            dk_all[:, cols] = (
                grad_key * key_cos - pltpu.roll(grad_key, half, 1) * key_sin
            ).astype(BF16)
        product = dot(dk_all[...], w[0], (1, 1)) + dot(dv_all[...], w[1], (1, 1))
        if turn == 0:
            total[...] = product
        else:
            product = total[...] + product
            for n in range(NEIGH):
                piece = product[n * NLEN:(n + 1) * NLEN].astype(BF16)
                part[:, n] = piece.reshape(NZ, ROWS, DE)


def on_core(kernel, name, shapes, near, *operands, scratch=()):
    return pl.pallas_call(
        kernel,
        out_shape=shapes,
        in_specs=[SMEM] + [VMEM] * len(operands),
        out_specs=jax.tree.map(lambda _: VMEM, shapes),
        scratch_shapes=scratch,
        compiler_params=pltpu.CompilerParams(vmem_limit_bytes=16 << 20),
        name=name,
    )(near, *operands)


def attention(*operands):
    width = operands[1].shape[2]
    return pl.pallas_call(
        attention_kernel,
        out_shape=(
            jax.ShapeDtypeStruct((NZ, NEIGH, ROWS, DE), BF16),
            jax.ShapeDtypeStruct((SPAN, width), BF16),
            jax.ShapeDtypeStruct((SPAN, width), BF16),
        ),
        in_specs=[VMEM] * len(operands),
        out_specs=(VMEM, VMEM, VMEM),
        scratch_shapes=[
            pltpu.VMEM((NEIGH * NLEN, width), BF16),
            pltpu.VMEM((NEIGH * NLEN, width), BF16),
            pltpu.VMEM((NEIGH * NLEN, DE), F32),
        ],
        compiler_params=pltpu.CompilerParams(vmem_limit_bytes=40 << 20),
        cost_estimate=pl.CostEstimate(
            flops=2_100_000_000, bytes_accessed=6_000_000, transcendentals=131072
        ),
        name="attention",
    )(*operands)


def local(queries, out_grad, encodings, kv_weight, neighbour_ids, rot_offset):
    x_at, c_at, z_at = lax.axis_index("x"), lax.axis_index("c"), lax.axis_index("z")
    spans = neighbour_ids.shape[0]
    reads = spans * NEIGH
    span_at = z_at % 2
    ids = neighbour_ids.reshape(reads)

    weight_pair = swapped(kv_weight, "z", NZ)
    rows_q = queries.reshape(spans, SPAN, -1)
    rows_g = out_grad.reshape(spans, SPAN, -1)
    other = jnp.concatenate(
        [
            lax.dynamic_index_in_dim(rows_q, 1 - span_at, 0, keepdims=False),
            lax.dynamic_index_in_dim(rows_g, 1 - span_at, 0, keepdims=False),
        ],
        axis=0,
    )
    q_own = lax.dynamic_index_in_dim(rows_q, span_at, 0, keepdims=False)
    g_own = lax.dynamic_index_in_dim(rows_g, span_at, 0, keepdims=False)
    offsets = lax.dynamic_index_in_dim(rot_offset, span_at, 0, keepdims=False)
    positions = offsets[:, None] + jnp.arange(NLEN, dtype=jnp.int32)[None, :]
    key_cos, key_sin = rotary_tables(positions.reshape(NEIGH * NLEN))
    query_cos, query_sin = rotary_tables(jnp.arange(SPAN, dtype=jnp.int32))

    near = [ids] + [shifted(ids, "x", NX, s) for s in range(1, NX)]
    near = jnp.concatenate(near + [x_at.reshape(1), c_at.reshape(1)])
    copies = jnp.broadcast_to(encodings, (NY, ROWS, DE))
    over_y = lax.all_to_all(copies, "y", split_axis=0, concat_axis=0, tiled=True)
    other, over_y = lax.optimization_barrier((other, over_y))
    beside = swapped(over_y, "c", NC)
    block = (reads, ROWS, DE)
    asked = on_core(
        pick_kernel, "pick", jax.ShapeDtypeStruct((NX, *block), BF16), near, over_y, beside
    )
    from_pair = swapped(other, "z", NZ)
    q_pair, g_pair = from_pair[:SPAN], from_pair[SPAN:]
    found = lax.all_to_all(asked, "x", split_axis=0, concat_axis=0, tiled=True)

    to_z = on_core(
        spread_kernel, "spread", jax.ShapeDtypeStruct((NZ, NEIGH, ROWS, DE), BF16), near, found
    )
    tok = lax.all_to_all(to_z, "z", split_axis=0, concat_axis=0, tiled=True)
    part, dq_own, dq_pair = attention(
        tok, kv_weight, weight_pair, q_own, q_pair, g_own, g_pair,
        key_cos, key_sin, query_cos, query_sin,
    )

    from_heads = lax.all_to_all(part, "z", split_axis=0, concat_axis=0, tiled=True)
    from_heads = from_heads.reshape(NZ // spans, spans, NEIGH, ROWS, DE)
    read_sum = jnp.sum(from_heads.astype(F32), axis=0).astype(BF16).reshape(reads, ROWS, DE)

    read_copies = jnp.broadcast_to(read_sum, (NX, *block))
    read_x = lax.all_to_all(read_copies, "x", split_axis=0, concat_axis=0, tiled=True)
    owners = (NY, ROWS, DE)
    mine, theirs = on_core(
        owner_kernel, "owner_sums",
        (jax.ShapeDtypeStruct(owners, F32), jax.ShapeDtypeStruct(owners, BF16)),
        near, read_x, scratch=[pltpu.VMEM((NC * NY, ROWS, DE), F32)],
    )
    owner_part = (mine + swapped(theirs, "c", NC).astype(F32)).astype(BF16)
    owner_part, dq_pair = lax.optimization_barrier((owner_part, dq_pair))
    from_y = lax.all_to_all(owner_part, "y", split_axis=0, concat_axis=0, tiled=True)
    owned = jnp.sum(from_y.astype(F32), axis=0)

    dq_back = swapped(dq_pair, "z", NZ)
    first = jnp.where(span_at == 0, dq_own, dq_back)
    second = jnp.where(span_at == 0, dq_back, dq_own)
    grad_query = jnp.concatenate([first, second], axis=0)
    return (grad_query, owned.reshape(1, ROWS, DE))


def solution(mesh):
    fine = Mesh(mesh.devices.reshape(NX, NY, NC, NZ), ("x", "y", "c", "z"))
    enc = ("x", "y", "c")
    in_specs = (
        P(enc, "z"),
        P(enc, "z"),
        P(enc, "z", None),
        P(None, None, "z"),
        P(enc, None),
        P(enc, None),
    )
    out_specs = (P(enc, "z"), P(enc, "z", None))
    return jax.shard_map(local, mesh=fine, in_specs=in_specs, out_specs=out_specs, check_vma=False)
```

```python
import math

import jax
import jax.numpy as jnp
from jax import lax
from jax.experimental import pallas as pl
from jax.experimental.pallas import tpu as pltpu
from jax.sharding import Mesh, PartitionSpec as P

HEAD = 128
DE = 896
SPAN = 64
NEIGH = 2
NLEN = 128
NX, NY, NC, NZ = 4, 8, 2, 8
ROWS = NLEN // NZ
F32, BF16 = jnp.float32, jnp.bfloat16
VMEM = pl.BlockSpec(memory_space=pltpu.VMEM)
SMEM = pl.BlockSpec(memory_space=pltpu.SMEM)
ANY = pl.BlockSpec(memory_space=pl.ANY)


def rotary_tables(positions):
    halfway = HEAD // 2
    exponent = jnp.arange(halfway, dtype=F32) * (2.0 / HEAD)
    frequency = jnp.exp(-math.log(10000.0) * exponent)
    angles = positions.astype(F32)[:, None] * frequency[None, :]
    cosine, sine = jnp.cos(angles), jnp.sin(angles)
    return jnp.concatenate([cosine, cosine], axis=-1), jnp.concatenate([-sine, sine], axis=-1)


def swapped(value, axis, size, bit=1):
    return lax.ppermute(value, axis, [(i, i ^ bit) for i in range(size)])


def dot(a, b, over=(1, 0)):
    return lax.dot_general(
        a, b, (((over[0],), (over[1],)), ((), ())), preferred_element_type=F32
    )


def near_id(near_ref, at_ref, column, read):
    return near_ref[jnp.bitwise_xor(at_ref[0], column), read // NEIGH, read % NEIGH]


def pick_kernel(near_ref, at_ref, mine_ref, theirs_ref, out_ref, sems):
    core, reads = at_ref[1], out_ref.shape[1]
    for column in range(NX):
        for read in range(reads):
            block = near_id(near_ref, at_ref, column, read)
            row, same = lax.rem(block // NC, NY), lax.rem(block, NC) == core
            sem = sems.at[column * reads + read]

            @pl.when(same)
            def _():
                pltpu.make_async_copy(mine_ref.at[row], out_ref.at[column, read], sem).start()

            @pl.when(jnp.logical_not(same))
            def _():
                pltpu.make_async_copy(theirs_ref.at[row], out_ref.at[column, read], sem).start()

    for column in range(NX):
        for read in range(reads):
            sem = sems.at[column * reads + read]
            pltpu.make_async_copy(mine_ref.at[0], out_ref.at[column, read], sem).wait()


def spread_kernel(near_ref, at_ref, from_ref, out_ref, sems):
    reads = from_ref.shape[1]
    spans = reads // NEIGH
    copies = []
    for read in range(reads):
        column = near_ref[0, read // NEIGH, read % NEIGH] // (NY * NC)
        for at in range(read // NEIGH, NZ, spans):
            copies.append(
                pltpu.make_async_copy(
                    from_ref.at[column, read], out_ref.at[at, read % NEIGH], sems.at[len(copies)]
                )
            )
            copies[-1].start()
    for copy in copies:
        copy.wait()


def owner_kernel(near_ref, at_ref, from_ref, mine_ref, theirs_ref, total):
    total[...] = jnp.zeros_like(total)
    here, core = at_ref[0], at_ref[1]
    for column in range(NX):
        for read in range(from_ref.shape[1]):
            block = near_id(near_ref, at_ref, column, read)

            @pl.when(block // (NY * NC) == here)
            def _():
                side = jnp.where(lax.rem(block, NC) == core, 0, NY)
                at = side + lax.rem(block // NC, NY)
                total[at] = total[at] + from_ref[column, read].astype(F32)

    mine_ref[...] = total[:NY]
    theirs_ref[...] = total[NY:].astype(BF16)


def attention_kernel(
    at_ref, tok, w_own, q_own, g_own, kc, ks, qc, qs, near_pair, far_pair,
    part, dq_own, dq_pair, dk_all, dv_all, total, w_pair, q_pair, g_pair, sems,
):
    core, depth = at_ref[1], w_own.shape[1]
    fetches = [
        pltpu.make_async_copy(near_pair.at[:depth], w_pair.at[core], sems.at[0]),
        pltpu.make_async_copy(far_pair.at[:depth], w_pair.at[1 - core], sems.at[1]),
        pltpu.make_async_copy(near_pair.at[depth:depth + SPAN], q_pair, sems.at[2]),
        pltpu.make_async_copy(near_pair.at[depth + SPAN:], g_pair, sems.at[3]),
    ]
    for fetch in fetches:
        fetch.start()
    scale = 1.0 / math.sqrt(HEAD)
    rows = jnp.concatenate([tok[:, n].reshape(NLEN, DE) for n in range(NEIGH)], axis=0)
    key_cos, key_sin, query_cos, query_sin = kc[...], ks[...], qc[...], qs[...]
    half = HEAD // 2
    for turn, (w, q, g, dq) in enumerate(
        ((w_own, q_own, g_own, dq_own), (w_pair, q_pair, g_pair, dq_pair))
    ):
        if turn == 1:
            for fetch in fetches:
                fetch.wait()
        key_raw = dot(rows, w[0])
        values = dot(rows, w[1]).astype(BF16)
        for head in range(w.shape[2] // HEAD):
            cols = slice(head * HEAD, (head + 1) * HEAD)
            raw = key_raw[:, cols]
            key = (raw * key_cos + pltpu.roll(raw, half, 1) * key_sin).astype(BF16)
            value = values[:, cols]
            wide = q[:, cols].astype(F32)
            query = (wide * query_cos + pltpu.roll(wide, half, 1) * query_sin).astype(BF16)
            grad = g[:, cols]
            exponentials = jnp.exp(dot(query, key, (1, 1)) * scale)
            weights = exponentials / jnp.sum(exponentials, axis=-1, keepdims=True)
            weights_low = weights.astype(BF16)
            grad_weights = dot(grad, value, (1, 1))
            delta = jnp.sum(weights_low.astype(F32) * grad_weights, axis=-1, keepdims=True)
            grad_scores = (weights * (grad_weights - delta) * scale).astype(BF16)
            dv_all[:, cols] = dot(weights_low, grad, (0, 0)).astype(BF16)
            grad_query = dot(grad_scores, key)
            dq[:, cols] = (
                grad_query * query_cos - pltpu.roll(grad_query, half, 1) * query_sin
            ).astype(BF16)
            grad_key = dot(grad_scores, query, (0, 0))
            dk_all[:, cols] = (
                grad_key * key_cos - pltpu.roll(grad_key, half, 1) * key_sin
            ).astype(BF16)
        product = dot(dk_all[...], w[0], (1, 1)) + dot(dv_all[...], w[1], (1, 1))
        if turn == 0:
            total[...] = product
        else:
            product = total[...] + product
            for n in range(NEIGH):
                piece = product[n * NLEN:(n + 1) * NLEN].astype(BF16)
                part[:, n] = piece.reshape(NZ, ROWS, DE)


def on_core(kernel, name, shapes, scalars, *operands, scratch=(), space=VMEM):
    return pl.pallas_call(
        kernel,
        out_shape=shapes,
        in_specs=[SMEM] * len(scalars) + [space] * len(operands),
        out_specs=jax.tree.map(lambda _: space, shapes),
        scratch_shapes=scratch,
        compiler_params=pltpu.CompilerParams(vmem_limit_bytes=16 << 20),
        name=name,
    )(*scalars, *operands)


def attention(at, *operands):
    _, depth, width = operands[1].shape
    return pl.pallas_call(
        attention_kernel,
        out_shape=(
            jax.ShapeDtypeStruct((NZ, NEIGH, ROWS, DE), BF16),
            jax.ShapeDtypeStruct((SPAN, width), BF16),
            jax.ShapeDtypeStruct((SPAN, width), BF16),
        ),
        in_specs=[SMEM] + [VMEM] * (len(operands) - 2) + [ANY] * 2,
        out_specs=(VMEM, VMEM, VMEM),
        scratch_shapes=[
            pltpu.VMEM((NEIGH * NLEN, width), BF16),
            pltpu.VMEM((NEIGH * NLEN, width), BF16),
            pltpu.VMEM((NEIGH * NLEN, DE), F32),
            pltpu.VMEM((2, depth, width), BF16),
            pltpu.VMEM((SPAN, width), BF16),
            pltpu.VMEM((SPAN, width), BF16),
            pltpu.SemaphoreType.DMA((4,)),
        ],
        compiler_params=pltpu.CompilerParams(vmem_limit_bytes=40 << 20),
        cost_estimate=pl.CostEstimate(
            flops=2_100_000_000, bytes_accessed=6_000_000, transcendentals=131072
        ),
        name="attention",
    )(at, *operands)


def local(queries, out_grad, encodings, kv_weight, neighbour_ids, rot_offset):
    x_at, c_at, z_at = lax.axis_index("x"), lax.axis_index("c"), lax.axis_index("z")
    spans = neighbour_ids.shape[0]
    reads = spans * NEIGH
    span_at = z_at % 2

    rows_q = queries.reshape(spans, SPAN, -1)
    rows_g = out_grad.reshape(spans, SPAN, -1)
    to_pair = jnp.concatenate(
        [
            lax.dynamic_index_in_dim(kv_weight, c_at, 0, keepdims=False),
            lax.dynamic_index_in_dim(rows_q, 1 - span_at, 0, keepdims=False),
            lax.dynamic_index_in_dim(rows_g, 1 - span_at, 0, keepdims=False),
        ],
        axis=0,
    )
    near_pair = swapped(to_pair, "z", NZ)
    q_own = lax.dynamic_index_in_dim(rows_q, span_at, 0, keepdims=False)
    g_own = lax.dynamic_index_in_dim(rows_g, span_at, 0, keepdims=False)
    offsets = lax.dynamic_index_in_dim(rot_offset, span_at, 0, keepdims=False)
    positions = offsets[:, None] + jnp.arange(NLEN, dtype=jnp.int32)[None, :]
    key_cos, key_sin = rotary_tables(positions.reshape(NEIGH * NLEN))
    query_cos, query_sin = rotary_tables(jnp.arange(SPAN, dtype=jnp.int32))

    at = jnp.stack([x_at, c_at])
    near = jnp.stack([neighbour_ids, swapped(neighbour_ids, "x", NX)])
    near = jnp.concatenate([near, swapped(near, "x", NX, 2)])
    copies = jnp.broadcast_to(encodings, (NY, ROWS, DE))
    over_y = lax.all_to_all(copies, "y", split_axis=0, concat_axis=0, tiled=True)
    over_y, near = lax.optimization_barrier((over_y, near))
    beside = swapped(over_y, "c", NC)
    block = (reads, ROWS, DE)
    asked = on_core(
        pick_kernel, "pick", jax.ShapeDtypeStruct((NX, *block), BF16), (near, at),
        over_y, beside, scratch=[pltpu.SemaphoreType.DMA((NX * reads,))], space=ANY,
    )
    found = lax.all_to_all(asked, "x", split_axis=0, concat_axis=0, tiled=True)

    to_z = on_core(
        spread_kernel, "spread", jax.ShapeDtypeStruct((NZ, NEIGH, ROWS, DE), BF16), (near, at),
        found, scratch=[pltpu.SemaphoreType.DMA((NZ * NEIGH,))], space=ANY,
    )
    to_z, near_pair = lax.optimization_barrier((to_z, near_pair))
    tok = lax.all_to_all(to_z, "z", split_axis=0, concat_axis=0, tiled=True)
    far_pair = swapped(near_pair, "c", NC)
    part, dq_own, dq_pair = attention(
        at, tok, kv_weight, q_own, g_own, key_cos, key_sin, query_cos, query_sin,
        near_pair, far_pair,
    )

    from_heads = lax.all_to_all(part, "z", split_axis=0, concat_axis=0, tiled=True)
    dq_back = swapped(dq_pair, "z", NZ)
    from_heads, dq_back = lax.optimization_barrier((from_heads, dq_back))
    from_heads = from_heads.reshape(NZ // spans, spans, NEIGH, ROWS, DE)
    read_sum = jnp.sum(from_heads.astype(F32), axis=0).astype(BF16).reshape(reads, ROWS, DE)

    read_copies = jnp.broadcast_to(read_sum, (NX, *block))
    read_x = lax.all_to_all(read_copies, "x", split_axis=0, concat_axis=0, tiled=True)
    owners = (NY, ROWS, DE)
    mine, theirs = on_core(
        owner_kernel, "owner_sums",
        (jax.ShapeDtypeStruct(owners, F32), jax.ShapeDtypeStruct(owners, BF16)),
        (near, at), read_x, scratch=[pltpu.VMEM((NC * NY, ROWS, DE), F32)],
    )
    owner_part = (mine + swapped(theirs, "c", NC).astype(F32)).astype(BF16)
    from_y = lax.all_to_all(owner_part, "y", split_axis=0, concat_axis=0, tiled=True)
    owned = jnp.sum(from_y.astype(F32), axis=0)

    first = jnp.where(span_at == 0, dq_own, dq_back)
    second = jnp.where(span_at == 0, dq_back, dq_own)
    grad_query = jnp.concatenate([first, second], axis=0)
    return (grad_query, owned.reshape(1, ROWS, DE))


def solution(mesh):
    fine = Mesh(mesh.devices.reshape(NX, NY, NC, NZ), ("x", "y", "c", "z"))
    enc = ("x", "y", "c")
    in_specs = (
        P(enc, "z"),
        P(enc, "z"),
        P(enc, "z", None),
        P(None, None, "z"),
        P(enc, None),
        P(enc, None),
    )
    out_specs = (P(enc, "z"), P(enc, "z", None))
    return jax.shard_map(local, mesh=fine, in_specs=in_specs, out_specs=out_specs, check_vma=False)
```

```python
import math

import jax
import jax.numpy as jnp
from jax import lax
from jax.experimental import pallas as pl
from jax.experimental.pallas import tpu as pltpu
from jax.sharding import Mesh, PartitionSpec as P

HEAD = 128
DE = 896
SPAN = 64
NEIGH = 2
NLEN = 128
NX, NY, NC, NZ = 4, 8, 2, 8
ROWS = NLEN // NZ
F32, BF16 = jnp.float32, jnp.bfloat16
VMEM = pl.BlockSpec(memory_space=pltpu.VMEM)
SMEM = pl.BlockSpec(memory_space=pltpu.SMEM)
ANY = pl.BlockSpec(memory_space=pl.ANY)


def rotary_tables(positions):
    halfway = HEAD // 2
    exponent = jnp.arange(halfway, dtype=F32) * (2.0 / HEAD)
    frequency = jnp.exp(-math.log(10000.0) * exponent)
    angles = positions.astype(F32)[:, None] * frequency[None, :]
    cosine, sine = jnp.cos(angles), jnp.sin(angles)
    return jnp.concatenate([cosine, cosine], axis=-1), jnp.concatenate([-sine, sine], axis=-1)


def shifted(value, axis, size, shift):
    return lax.ppermute(value, axis, [(i, (i + shift) % size) for i in range(size)])


def swapped(value, axis, size):
    return lax.ppermute(value, axis, [(i, i ^ 1) for i in range(size)])


def dot(a, b, over=(1, 0)):
    return lax.dot_general(
        a, b, (((over[0],), (over[1],)), ((), ())), preferred_element_type=F32
    )


def near_id(near_ref, at_ref, column, read):
    return near_ref[lax.rem(at_ref[0] - column + NX, NX), read // NEIGH, read % NEIGH]


def pick_kernel(near_ref, at_ref, mine_ref, theirs_ref, out_ref, sems):
    core, reads = at_ref[1], out_ref.shape[1]
    for column in range(NX):
        for read in range(reads):
            block = near_id(near_ref, at_ref, column, read)
            row, same = lax.rem(block // NC, NY), lax.rem(block, NC) == core
            sem = sems.at[column * reads + read]

            @pl.when(same)
            def _():
                pltpu.make_async_copy(mine_ref.at[row], out_ref.at[column, read], sem).start()

            @pl.when(jnp.logical_not(same))
            def _():
                pltpu.make_async_copy(theirs_ref.at[row], out_ref.at[column, read], sem).start()

    for column in range(NX):
        for read in range(reads):
            sem = sems.at[column * reads + read]
            pltpu.make_async_copy(mine_ref.at[0], out_ref.at[column, read], sem).wait()


def spread_kernel(near_ref, at_ref, from_ref, out_ref):
    reads = from_ref.shape[1]
    spans = reads // NEIGH
    for read in range(reads):
        owner = near_ref[0, read // NEIGH, read % NEIGH]
        block = from_ref[owner // (NY * NC), read]
        for at in range(read // NEIGH, NZ, spans):
            out_ref[at, read % NEIGH] = block


def owner_kernel(near_ref, at_ref, from_ref, mine_ref, theirs_ref, total):
    total[...] = jnp.zeros_like(total)
    here, core = at_ref[0], at_ref[1]
    for column in range(NX):
        for read in range(from_ref.shape[1]):
            block = near_id(near_ref, at_ref, column, read)

            @pl.when(block // (NY * NC) == here)
            def _():
                side = jnp.where(lax.rem(block, NC) == core, 0, NY)
                at = side + lax.rem(block // NC, NY)
                total[at] = total[at] + from_ref[column, read].astype(F32)

    mine_ref[...] = total[:NY]
    theirs_ref[...] = total[NY:].astype(BF16)


def attention_kernel(
    tok, w_own, q_own, g_own, q_pair, g_pair, kc, ks, qc, qs, w_far,
    part, dq_own, dq_pair, dk_all, dv_all, w_pair, sem,
):
    fetch = pltpu.make_async_copy(w_far, w_pair, sem)
    fetch.start()
    scale = 1.0 / math.sqrt(HEAD)
    half = HEAD // 2
    width = w_own.shape[2]
    rows = jnp.concatenate([tok[:, n].reshape(NLEN, DE) for n in range(NEIGH)], axis=0)
    projected = [(dot(rows, w_own[0]), dot(rows, w_own[1]).astype(BF16))]
    fetch.wait()
    projected.append((dot(rows, w_pair[0]), dot(rows, w_pair[1]).astype(BF16)))
    key_cos, key_sin, query_cos, query_sin = kc[...], ks[...], qc[...], qs[...]
    for turn, (q, g, dq) in enumerate(((q_own, g_own, dq_own), (q_pair, g_pair, dq_pair))):
        key_raw, values = projected[turn]
        for head in range(width // HEAD):
            cols = slice(head * HEAD, (head + 1) * HEAD)
            place = slice(turn * width + head * HEAD, turn * width + (head + 1) * HEAD)
            raw = key_raw[:, cols]
            key = (raw * key_cos + pltpu.roll(raw, half, 1) * key_sin).astype(BF16)
            value = values[:, cols]
            wide = q[:, cols].astype(F32)
            query = (wide * query_cos + pltpu.roll(wide, half, 1) * query_sin).astype(BF16)
            grad = g[:, cols]
            exponentials = jnp.exp(dot(query, key, (1, 1)) * scale)
            weights = exponentials / jnp.sum(exponentials, axis=-1, keepdims=True)
            weights_low = weights.astype(BF16)
            grad_weights = dot(grad, value, (1, 1))
            delta = jnp.sum(weights_low.astype(F32) * grad_weights, axis=-1, keepdims=True)
            grad_scores = (weights * (grad_weights - delta) * scale).astype(BF16)
            dv_all[:, place] = dot(weights_low, grad, (0, 0)).astype(BF16)
            grad_query = dot(grad_scores, key)
            dq[:, cols] = (
                grad_query * query_cos - pltpu.roll(grad_query, half, 1) * query_sin
            ).astype(BF16)
            grad_key = dot(grad_scores, query, (0, 0))
            dk_all[:, place] = (
                grad_key * key_cos - pltpu.roll(grad_key, half, 1) * key_sin
            ).astype(BF16)
    product = dot(dk_all[:, :width], w_own[0], (1, 1)) + dot(dv_all[:, :width], w_own[1], (1, 1))
    product = product + dot(dk_all[:, width:], w_pair[0], (1, 1))
    product = product + dot(dv_all[:, width:], w_pair[1], (1, 1))
    for n in range(NEIGH):
        piece = product[n * NLEN:(n + 1) * NLEN].astype(BF16)
        part[:, n] = piece.reshape(NZ, ROWS, DE)


def on_core(kernel, name, shapes, scalars, *operands, scratch=(), space=VMEM):
    return pl.pallas_call(
        kernel,
        out_shape=shapes,
        in_specs=[SMEM] * len(scalars) + [space] * len(operands),
        out_specs=jax.tree.map(lambda _: space, shapes),
        scratch_shapes=scratch,
        compiler_params=pltpu.CompilerParams(vmem_limit_bytes=16 << 20),
        name=name,
    )(*scalars, *operands)


def attention(*operands):
    _, depth, width = operands[1].shape
    return pl.pallas_call(
        attention_kernel,
        out_shape=(
            jax.ShapeDtypeStruct((NZ, NEIGH, ROWS, DE), BF16),
            jax.ShapeDtypeStruct((SPAN, width), BF16),
            jax.ShapeDtypeStruct((SPAN, width), BF16),
        ),
        in_specs=[VMEM] * (len(operands) - 1) + [ANY],
        out_specs=(VMEM, VMEM, VMEM),
        scratch_shapes=[
            pltpu.VMEM((NEIGH * NLEN, 2 * width), BF16),
            pltpu.VMEM((NEIGH * NLEN, 2 * width), BF16),
            pltpu.VMEM((2, depth, width), BF16),
            pltpu.SemaphoreType.DMA,
        ],
        compiler_params=pltpu.CompilerParams(vmem_limit_bytes=40 << 20),
        cost_estimate=pl.CostEstimate(
            flops=2_100_000_000, bytes_accessed=6_000_000, transcendentals=131072
        ),
        name="attention",
    )(*operands)


def local(queries, out_grad, encodings, kv_weight, neighbour_ids, rot_offset):
    x_at, c_at, z_at = lax.axis_index("x"), lax.axis_index("c"), lax.axis_index("z")
    spans = neighbour_ids.shape[0]
    reads = spans * NEIGH
    span_at = z_at % 2

    w_far = swapped(kv_weight, "z", NZ)
    rows_q = queries.reshape(spans, SPAN, -1)
    rows_g = out_grad.reshape(spans, SPAN, -1)
    other = jnp.concatenate(
        [
            lax.dynamic_index_in_dim(rows_q, 1 - span_at, 0, keepdims=False),
            lax.dynamic_index_in_dim(rows_g, 1 - span_at, 0, keepdims=False),
        ],
        axis=0,
    )
    q_own = lax.dynamic_index_in_dim(rows_q, span_at, 0, keepdims=False)
    g_own = lax.dynamic_index_in_dim(rows_g, span_at, 0, keepdims=False)
    offsets = lax.dynamic_index_in_dim(rot_offset, span_at, 0, keepdims=False)
    positions = offsets[:, None] + jnp.arange(NLEN, dtype=jnp.int32)[None, :]
    key_cos, key_sin = rotary_tables(positions.reshape(NEIGH * NLEN))
    query_cos, query_sin = rotary_tables(jnp.arange(SPAN, dtype=jnp.int32))

    at = jnp.stack([x_at, c_at])
    near = [neighbour_ids] + [shifted(neighbour_ids, "x", NX, s) for s in range(1, NX)]
    near = jnp.stack(near)
    copies = jnp.broadcast_to(encodings, (NY, ROWS, DE))
    over_y = lax.all_to_all(copies, "y", split_axis=0, concat_axis=0, tiled=True)
    over_y, near, other = lax.optimization_barrier((over_y, near, other))
    beside = swapped(over_y, "c", NC)
    block = (reads, ROWS, DE)
    asked = on_core(
        pick_kernel, "pick", jax.ShapeDtypeStruct((NX, *block), BF16), (near, at),
        over_y, beside, scratch=[pltpu.SemaphoreType.DMA((NX * reads,))], space=ANY,
    )
    found = lax.all_to_all(asked, "x", split_axis=0, concat_axis=0, tiled=True)

    to_z = on_core(
        spread_kernel, "spread", jax.ShapeDtypeStruct((NZ, NEIGH, ROWS, DE), BF16), (near, at),
        found,
    )
    to_z, w_far = lax.optimization_barrier((to_z, w_far))
    tok = lax.all_to_all(to_z, "z", split_axis=0, concat_axis=0, tiled=True)
    from_pair = swapped(other, "z", NZ)
    part, dq_own, dq_pair = attention(
        tok, kv_weight, q_own, g_own, from_pair[:SPAN], from_pair[SPAN:],
        key_cos, key_sin, query_cos, query_sin, w_far,
    )

    from_heads = lax.all_to_all(part, "z", split_axis=0, concat_axis=0, tiled=True)
    from_heads = from_heads.reshape(NZ // spans, spans, NEIGH, ROWS, DE)
    read_sum = jnp.sum(from_heads.astype(F32), axis=0).astype(BF16).reshape(reads, ROWS, DE)

    read_copies = jnp.broadcast_to(read_sum, (NX, *block))
    read_x = lax.all_to_all(read_copies, "x", split_axis=0, concat_axis=0, tiled=True)
    owners = (NY, ROWS, DE)
    mine, theirs = on_core(
        owner_kernel, "owner_sums",
        (jax.ShapeDtypeStruct(owners, F32), jax.ShapeDtypeStruct(owners, BF16)),
        (near, at), read_x, scratch=[pltpu.VMEM((NC * NY, ROWS, DE), F32)],
    )
    owner_part = (mine + swapped(theirs, "c", NC).astype(F32)).astype(BF16)
    owner_part, dq_pair = lax.optimization_barrier((owner_part, dq_pair))
    dq_back = swapped(dq_pair, "z", NZ)
    from_y = lax.all_to_all(owner_part, "y", split_axis=0, concat_axis=0, tiled=True)
    owned = jnp.sum(from_y.astype(F32), axis=0)

    first = jnp.where(span_at == 0, dq_own, dq_back)
    second = jnp.where(span_at == 0, dq_back, dq_own)
    grad_query = jnp.concatenate([first, second], axis=0)
    return (grad_query, owned.reshape(1, ROWS, DE))


def solution(mesh):
    fine = Mesh(mesh.devices.reshape(NX, NY, NC, NZ), ("x", "y", "c", "z"))
    enc = ("x", "y", "c")
    in_specs = (
        P(enc, "z"),
        P(enc, "z"),
        P(enc, "z", None),
        P(None, None, "z"),
        P(enc, None),
        P(enc, None),
    )
    out_specs = (P(enc, "z"), P(enc, "z", None))
    return jax.shard_map(local, mesh=fine, in_specs=in_specs, out_specs=out_specs, check_vma=False)
```

```python
import math

import jax
import jax.numpy as jnp
from jax import lax
from jax.experimental import pallas as pl
from jax.experimental.pallas import tpu as pltpu
from jax.sharding import Mesh, PartitionSpec as P

HEAD = 128
DE = 896
SPAN = 64
NEIGH = 2
NLEN = 128
NX, NY, NC, NZ = 4, 8, 2, 8
ROWS = NLEN // NZ
F32, BF16 = jnp.float32, jnp.bfloat16
VMEM = pl.BlockSpec(memory_space=pltpu.VMEM)
SMEM = pl.BlockSpec(memory_space=pltpu.SMEM)
ANY = pl.BlockSpec(memory_space=pl.ANY)


def both_orders(major, count, minor, flip):
    return [[i * major for i in range(count)], [(i ^ flip) * major + minor for i in range(count)]]


FLIP_Y, FLIP_X, FLIP_Z = NY - 1, NX - 1, NZ - 2
GROUPS = {
    "y": (("y", "c"), both_orders(NC, NY, 1, FLIP_Y)),
    "x": (("x", "c"), both_orders(NC, NX, 1, FLIP_X)),
    "z": (("c", "z"), both_orders(1, NZ, NZ, FLIP_Z)),
}


def exchange(value, axis):
    axes, groups = GROUPS[axis]
    return lax.all_to_all(
        value, axes, split_axis=0, concat_axis=0, axis_index_groups=groups, tiled=True
    )


def rotary_tables(positions):
    halfway = HEAD // 2
    exponent = jnp.arange(halfway, dtype=F32) * (2.0 / HEAD)
    frequency = jnp.exp(-math.log(10000.0) * exponent)
    angles = positions.astype(F32)[:, None] * frequency[None, :]
    cosine, sine = jnp.cos(angles), jnp.sin(angles)
    return jnp.concatenate([cosine, cosine], axis=-1), jnp.concatenate([-sine, sine], axis=-1)


def shifted(value, axis, size, shift):
    return lax.ppermute(value, axis, [(i, (i + shift) % size) for i in range(size)])


def swapped(value, axis, size):
    return lax.ppermute(value, axis, [(i, i ^ 1) for i in range(size)])


def dot(a, b, over=(1, 0)):
    return lax.dot_general(
        a, b, (((over[0],), (over[1],)), ((), ())), preferred_element_type=F32
    )


def near_id(near_ref, at_ref, column, read):
    return near_ref[lax.rem(at_ref[0] - column + NX, NX), read // NEIGH, read % NEIGH]


def pick_kernel(near_ref, at_ref, mine_ref, theirs_ref, out_ref, sems):
    core, reads = at_ref[1], out_ref.shape[1]
    for column in range(NX):
        for read in range(reads):
            block = near_id(near_ref, at_ref, column ^ (FLIP_X * core), read)
            side = lax.rem(block, NC)
            row, same = lax.rem(block // NC, NY) ^ (FLIP_Y * side), side == core
            sem = sems.at[column * reads + read]

            @pl.when(same)
            def _():
                pltpu.make_async_copy(mine_ref.at[row], out_ref.at[column, read], sem).start()

            @pl.when(jnp.logical_not(same))
            def _():
                pltpu.make_async_copy(theirs_ref.at[row], out_ref.at[column, read], sem).start()

    for column in range(NX):
        for read in range(reads):
            sem = sems.at[column * reads + read]
            pltpu.make_async_copy(mine_ref.at[0], out_ref.at[column, read], sem).wait()


def spread_kernel(near_ref, at_ref, from_ref, out_ref):
    reads = from_ref.shape[1]
    spans = reads // NEIGH
    for read in range(reads):
        owner = near_ref[0, read // NEIGH, read % NEIGH]
        block = from_ref[(owner // (NY * NC)) ^ (FLIP_X * at_ref[1]), read]
        for at in range(read // NEIGH, NZ, spans):
            out_ref[at, read % NEIGH] = block


def owner_kernel(near_ref, at_ref, from_ref, mine_ref, theirs_ref, total):
    total[...] = jnp.zeros_like(total)
    here, core = at_ref[0], at_ref[1]
    for column in range(NX):
        for read in range(from_ref.shape[1]):
            block = near_id(near_ref, at_ref, column ^ (FLIP_X * core), read)

            @pl.when(block // (NY * NC) == here)
            def _():
                side = lax.rem(block, NC)
                row = lax.rem(block // NC, NY) ^ (FLIP_Y * side)
                at = jnp.where(side == core, 0, NY) + row
                total[at] = total[at] + from_ref[column, read].astype(F32)

    mine_ref[...] = total[:NY]
    theirs_ref[...] = total[NY:].astype(BF16)


def attention_kernel(
    tok, w_own, q_own, g_own, q_pair, g_pair, kc, ks, qc, qs, w_far,
    part, dq_own, dq_pair, dk_all, dv_all, w_pair, sem,
):
    fetch = pltpu.make_async_copy(w_far, w_pair, sem)
    fetch.start()
    scale = 1.0 / math.sqrt(HEAD)
    half = HEAD // 2
    width = w_own.shape[2]
    rows = jnp.concatenate([tok[:, n].reshape(NLEN, DE) for n in range(NEIGH)], axis=0)
    projected = [(dot(rows, w_own[0]), dot(rows, w_own[1]).astype(BF16))]
    fetch.wait()
    projected.append((dot(rows, w_pair[0]), dot(rows, w_pair[1]).astype(BF16)))
    key_cos, key_sin, query_cos, query_sin = kc[...], ks[...], qc[...], qs[...]
    for turn, (q, g, dq) in enumerate(((q_own, g_own, dq_own), (q_pair, g_pair, dq_pair))):
        key_raw, values = projected[turn]
        for head in range(width // HEAD):
            cols = slice(head * HEAD, (head + 1) * HEAD)
            place = slice(turn * width + head * HEAD, turn * width + (head + 1) * HEAD)
            raw = key_raw[:, cols]
            key = (raw * key_cos + pltpu.roll(raw, half, 1) * key_sin).astype(BF16)
            value = values[:, cols]
            wide = q[:, cols].astype(F32)
            query = (wide * query_cos + pltpu.roll(wide, half, 1) * query_sin).astype(BF16)
            grad = g[:, cols]
            exponentials = jnp.exp(dot(query, key, (1, 1)) * scale)
            weights = exponentials / jnp.sum(exponentials, axis=-1, keepdims=True)
            weights_low = weights.astype(BF16)
            grad_weights = dot(grad, value, (1, 1))
            delta = jnp.sum(weights_low.astype(F32) * grad_weights, axis=-1, keepdims=True)
            grad_scores = (weights * (grad_weights - delta) * scale).astype(BF16)
            dv_all[:, place] = dot(weights_low, grad, (0, 0)).astype(BF16)
            grad_query = dot(grad_scores, key)
            dq[:, cols] = (
                grad_query * query_cos - pltpu.roll(grad_query, half, 1) * query_sin
            ).astype(BF16)
            grad_key = dot(grad_scores, query, (0, 0))
            dk_all[:, place] = (
                grad_key * key_cos - pltpu.roll(grad_key, half, 1) * key_sin
            ).astype(BF16)
    product = dot(dk_all[:, :width], w_own[0], (1, 1)) + dot(dv_all[:, :width], w_own[1], (1, 1))
    product = product + dot(dk_all[:, width:], w_pair[0], (1, 1))
    product = product + dot(dv_all[:, width:], w_pair[1], (1, 1))
    for n in range(NEIGH):
        piece = product[n * NLEN:(n + 1) * NLEN].astype(BF16)
        part[:, n] = piece.reshape(NZ, ROWS, DE)


def on_core(kernel, name, shapes, scalars, *operands, scratch=(), space=VMEM):
    return pl.pallas_call(
        kernel,
        out_shape=shapes,
        in_specs=[SMEM] * len(scalars) + [space] * len(operands),
        out_specs=jax.tree.map(lambda _: space, shapes),
        scratch_shapes=scratch,
        compiler_params=pltpu.CompilerParams(vmem_limit_bytes=16 << 20),
        name=name,
    )(*scalars, *operands)


def attention(*operands):
    _, depth, width = operands[1].shape
    return pl.pallas_call(
        attention_kernel,
        out_shape=(
            jax.ShapeDtypeStruct((NZ, NEIGH, ROWS, DE), BF16),
            jax.ShapeDtypeStruct((SPAN, width), BF16),
            jax.ShapeDtypeStruct((SPAN, width), BF16),
        ),
        in_specs=[VMEM] * (len(operands) - 1) + [ANY],
        out_specs=(VMEM, VMEM, VMEM),
        scratch_shapes=[
            pltpu.VMEM((NEIGH * NLEN, 2 * width), BF16),
            pltpu.VMEM((NEIGH * NLEN, 2 * width), BF16),
            pltpu.VMEM((2, depth, width), BF16),
            pltpu.SemaphoreType.DMA,
        ],
        compiler_params=pltpu.CompilerParams(vmem_limit_bytes=40 << 20),
        cost_estimate=pl.CostEstimate(
            flops=2_100_000_000, bytes_accessed=6_000_000, transcendentals=131072
        ),
        name="attention",
    )(*operands)


def local(queries, out_grad, encodings, kv_weight, neighbour_ids, rot_offset):
    x_at, c_at, z_at = lax.axis_index("x"), lax.axis_index("c"), lax.axis_index("z")
    spans = neighbour_ids.shape[0]
    reads = spans * NEIGH
    span_at = z_at % 2

    w_far = swapped(kv_weight, "z", NZ)
    offsets = lax.dynamic_index_in_dim(rot_offset, span_at, 0, keepdims=False)
    slices = jnp.arange(NZ, dtype=jnp.int32) ^ (FLIP_Z * c_at)
    tokens = (slices[:, None] * ROWS + jnp.arange(ROWS, dtype=jnp.int32)[None, :]).reshape(NLEN)
    positions = offsets[:, None] + tokens[None, :]
    key_cos, key_sin = rotary_tables(positions.reshape(NEIGH * NLEN))
    query_cos, query_sin = rotary_tables(jnp.arange(SPAN, dtype=jnp.int32))

    at = jnp.stack([x_at, c_at])
    near = [neighbour_ids] + [shifted(neighbour_ids, "x", NX, s) for s in range(1, NX)]
    near = jnp.stack(near)
    copies = jnp.broadcast_to(encodings, (NY, ROWS, DE))
    over_y = exchange(copies, "y")
    over_y, near = lax.optimization_barrier((over_y, near))
    beside = swapped(over_y, "c", NC)
    block = (reads, ROWS, DE)
    asked = on_core(
        pick_kernel, "pick", jax.ShapeDtypeStruct((NX, *block), BF16), (near, at),
        over_y, beside, scratch=[pltpu.SemaphoreType.DMA((NX * reads,))], space=ANY,
    )
    asked, queries, out_grad = lax.optimization_barrier((asked, queries, out_grad))
    found = exchange(asked, "x")

    rows_q = queries.reshape(spans, SPAN, -1)
    rows_g = out_grad.reshape(spans, SPAN, -1)
    other = jnp.concatenate(
        [
            lax.dynamic_index_in_dim(rows_q, 1 - span_at, 0, keepdims=False),
            lax.dynamic_index_in_dim(rows_g, 1 - span_at, 0, keepdims=False),
        ],
        axis=0,
    )
    q_own = lax.dynamic_index_in_dim(rows_q, span_at, 0, keepdims=False)
    g_own = lax.dynamic_index_in_dim(rows_g, span_at, 0, keepdims=False)

    to_z = on_core(
        spread_kernel, "spread", jax.ShapeDtypeStruct((NZ, NEIGH, ROWS, DE), BF16), (near, at),
        found,
    )
    to_z, w_far = lax.optimization_barrier((to_z, w_far))
    tok = exchange(to_z, "z")
    from_pair = swapped(other, "z", NZ)
    part, dq_own, dq_pair = attention(
        tok, kv_weight, q_own, g_own, from_pair[:SPAN], from_pair[SPAN:],
        key_cos, key_sin, query_cos, query_sin, w_far,
    )

    from_heads = exchange(part, "z")
    from_heads = from_heads.reshape(NZ // spans, spans, NEIGH, ROWS, DE)
    read_sum = jnp.sum(from_heads.astype(F32), axis=0).astype(BF16).reshape(reads, ROWS, DE)

    read_copies = jnp.broadcast_to(read_sum, (NX, *block))
    read_x = exchange(read_copies, "x")
    owners = (NY, ROWS, DE)
    mine, theirs = on_core(
        owner_kernel, "owner_sums",
        (jax.ShapeDtypeStruct(owners, F32), jax.ShapeDtypeStruct(owners, BF16)),
        (near, at), read_x, scratch=[pltpu.VMEM((NC * NY, ROWS, DE), F32)],
    )
    owner_part = (mine + swapped(theirs, "c", NC).astype(F32)).astype(BF16)
    owner_part, dq_pair = lax.optimization_barrier((owner_part, dq_pair))
    dq_back = swapped(dq_pair, "z", NZ)
    from_y = exchange(owner_part, "y")
    owned = jnp.sum(from_y.astype(F32), axis=0)

    first = jnp.where(span_at == 0, dq_own, dq_back)
    second = jnp.where(span_at == 0, dq_back, dq_own)
    grad_query = jnp.concatenate([first, second], axis=0)
    return (grad_query, owned.reshape(1, ROWS, DE))


def solution(mesh):
    fine = Mesh(mesh.devices.reshape(NX, NY, NC, NZ), ("x", "y", "c", "z"))
    enc = ("x", "y", "c")
    in_specs = (
        P(enc, "z"),
        P(enc, "z"),
        P(enc, "z", None),
        P(None, None, "z"),
        P(enc, None),
        P(enc, None),
    )
    out_specs = (P(enc, "z"), P(enc, "z", None))
    return jax.shard_map(local, mesh=fine, in_specs=in_specs, out_specs=out_specs, check_vma=False)
```

```python
import math

import jax
import jax.numpy as jnp
from jax import lax
from jax.experimental import pallas as pl
from jax.experimental.pallas import tpu as pltpu
from jax.sharding import Mesh, PartitionSpec as P

HEAD = 128
DE = 896
SPAN = 64
NEIGH = 2
NLEN = 128
NX, NY, NC, NZ = 4, 8, 2, 8
ROWS = NLEN // NZ
F32, BF16 = jnp.float32, jnp.bfloat16
VMEM = pl.BlockSpec(memory_space=pltpu.VMEM)
SMEM = pl.BlockSpec(memory_space=pltpu.SMEM)
ANY = pl.BlockSpec(memory_space=pl.ANY)


def rotary_tables(positions):
    halfway = HEAD // 2
    exponent = jnp.arange(halfway, dtype=F32) * (2.0 / HEAD)
    frequency = jnp.exp(-math.log(10000.0) * exponent)
    angles = positions.astype(F32)[:, None] * frequency[None, :]
    cosine, sine = jnp.cos(angles), jnp.sin(angles)
    return jnp.concatenate([cosine, cosine], axis=-1), jnp.concatenate([-sine, sine], axis=-1)


def exchange(value, axis):
    return lax.all_to_all(value, axis, split_axis=0, concat_axis=0, tiled=True)


def swapped(value, axis, size):
    return lax.ppermute(value, axis, [(i, i ^ 1) for i in range(size)])


def dot(a, b, over=(1, 0)):
    return lax.dot_general(
        a, b, (((over[0],), (over[1],)), ((), ())), preferred_element_type=F32
    )


def seat(block):
    return lax.div(block, NC)


def pick_kernel(ids_ref, from_ref, out_ref, sems):
    copies = []
    for read in range(out_ref.shape[0]):
        block = ids_ref[1, read // NEIGH, read % NEIGH]
        copies.append(
            pltpu.make_async_copy(from_ref.at[seat(block)], out_ref.at[read], sems.at[read])
        )
        copies[-1].start()
    for copy in copies:
        copy.wait()


def spread_kernel(ids_ref, core_ref, mine_ref, theirs_ref, out_ref, sems):
    reads = theirs_ref.shape[0]
    spans = reads // NEIGH
    places = [(read, at) for read in range(reads) for at in range(read // NEIGH, NZ, spans)]
    for count, (read, at) in enumerate(places):
        block = ids_ref[0, read // NEIGH, read % NEIGH]
        target, same = out_ref.at[at, read % NEIGH], lax.rem(block, NC) == core_ref[0]

        @pl.when(same)
        def _():
            pltpu.make_async_copy(mine_ref.at[seat(block)], target, sems.at[count]).start()

        @pl.when(jnp.logical_not(same))
        def _():
            pltpu.make_async_copy(theirs_ref.at[read], target, sems.at[count]).start()

    for count, (read, at) in enumerate(places):
        target = out_ref.at[at, read % NEIGH]
        pltpu.make_async_copy(theirs_ref.at[read], target, sems.at[count]).wait()


def owner_kernel(ids_ref, core_ref, mine_ref, theirs_ref, out_ref, total):
    total[...] = jnp.zeros_like(total)
    for side, reads_ref in enumerate((mine_ref, theirs_ref)):
        for read in range(reads_ref.shape[0]):
            block = ids_ref[side, read // NEIGH, read % NEIGH]

            @pl.when(lax.rem(block, NC) == core_ref[0])
            def _():
                at = seat(block)
                total[at] = total[at] + reads_ref[read].astype(F32)

    out_ref[...] = total[...].astype(BF16)


def attention_kernel(
    tok, w_own, q_own, g_own, q_pair, g_pair, kc, ks, qc, qs, w_far,
    part, dq_own, dq_pair, dk_all, dv_all, w_pair, sem,
):
    fetch = pltpu.make_async_copy(w_far, w_pair, sem)
    fetch.start()
    scale = 1.0 / math.sqrt(HEAD)
    half = HEAD // 2
    width = w_own.shape[2]
    rows = jnp.concatenate([tok[:, n].reshape(NLEN, DE) for n in range(NEIGH)], axis=0)
    projected = [(dot(rows, w_own[0]), dot(rows, w_own[1]).astype(BF16))]
    fetch.wait()
    projected.append((dot(rows, w_pair[0]), dot(rows, w_pair[1]).astype(BF16)))
    key_cos, key_sin, query_cos, query_sin = kc[...], ks[...], qc[...], qs[...]
    for turn, (q, g, dq) in enumerate(((q_own, g_own, dq_own), (q_pair, g_pair, dq_pair))):
        key_raw, values = projected[turn]
        for head in range(width // HEAD):
            cols = slice(head * HEAD, (head + 1) * HEAD)
            place = slice(turn * width + head * HEAD, turn * width + (head + 1) * HEAD)
            raw = key_raw[:, cols]
            key = (raw * key_cos + pltpu.roll(raw, half, 1) * key_sin).astype(BF16)
            value = values[:, cols]
            wide = q[:, cols].astype(F32)
            query = (wide * query_cos + pltpu.roll(wide, half, 1) * query_sin).astype(BF16)
            grad = g[:, cols]
            exponentials = jnp.exp(dot(query, key, (1, 1)) * scale)
            weights = exponentials / jnp.sum(exponentials, axis=-1, keepdims=True)
            weights_low = weights.astype(BF16)
            grad_weights = dot(grad, value, (1, 1))
            delta = jnp.sum(weights_low.astype(F32) * grad_weights, axis=-1, keepdims=True)
            grad_scores = (weights * (grad_weights - delta) * scale).astype(BF16)
            dv_all[:, place] = dot(weights_low, grad, (0, 0)).astype(BF16)
            grad_query = dot(grad_scores, key)
            dq[:, cols] = (
                grad_query * query_cos - pltpu.roll(grad_query, half, 1) * query_sin
            ).astype(BF16)
            grad_key = dot(grad_scores, query, (0, 0))
            dk_all[:, place] = (
                grad_key * key_cos - pltpu.roll(grad_key, half, 1) * key_sin
            ).astype(BF16)
    product = dot(dk_all[:, :width], w_own[0], (1, 1)) + dot(dv_all[:, :width], w_own[1], (1, 1))
    product = product + dot(dk_all[:, width:], w_pair[0], (1, 1))
    product = product + dot(dv_all[:, width:], w_pair[1], (1, 1))
    for n in range(NEIGH):
        piece = product[n * NLEN:(n + 1) * NLEN].astype(BF16)
        part[:, n] = piece.reshape(NZ, ROWS, DE)


def on_core(kernel, name, shapes, scalars, *operands, scratch=(), space=VMEM):
    return pl.pallas_call(
        kernel,
        out_shape=shapes,
        in_specs=[SMEM] * len(scalars) + [space] * len(operands),
        out_specs=jax.tree.map(lambda _: space, shapes),
        scratch_shapes=scratch,
        compiler_params=pltpu.CompilerParams(vmem_limit_bytes=16 << 20),
        name=name,
    )(*scalars, *operands)


def attention(*operands):
    _, depth, width = operands[1].shape
    return pl.pallas_call(
        attention_kernel,
        out_shape=(
            jax.ShapeDtypeStruct((NZ, NEIGH, ROWS, DE), BF16),
            jax.ShapeDtypeStruct((SPAN, width), BF16),
            jax.ShapeDtypeStruct((SPAN, width), BF16),
        ),
        in_specs=[VMEM] * (len(operands) - 1) + [ANY],
        out_specs=(VMEM, VMEM, VMEM),
        scratch_shapes=[
            pltpu.VMEM((NEIGH * NLEN, 2 * width), BF16),
            pltpu.VMEM((NEIGH * NLEN, 2 * width), BF16),
            pltpu.VMEM((2, depth, width), BF16),
            pltpu.SemaphoreType.DMA,
        ],
        compiler_params=pltpu.CompilerParams(vmem_limit_bytes=40 << 20),
        cost_estimate=pl.CostEstimate(
            flops=2_100_000_000, bytes_accessed=6_000_000, transcendentals=131072
        ),
        name="attention",
    )(*operands)


def local(queries, out_grad, encodings, kv_weight, neighbour_ids, rot_offset):
    c_at, z_at = lax.axis_index("c"), lax.axis_index("z")
    spans = neighbour_ids.shape[0]
    reads = spans * NEIGH
    span_at = z_at % 2

    w_far = swapped(kv_weight, "z", NZ)
    rows_q = queries.reshape(spans, SPAN, -1)
    rows_g = out_grad.reshape(spans, SPAN, -1)
    other = jnp.concatenate(
        [
            lax.dynamic_index_in_dim(rows_q, 1 - span_at, 0, keepdims=False),
            lax.dynamic_index_in_dim(rows_g, 1 - span_at, 0, keepdims=False),
        ],
        axis=0,
    )
    q_own = lax.dynamic_index_in_dim(rows_q, span_at, 0, keepdims=False)
    g_own = lax.dynamic_index_in_dim(rows_g, span_at, 0, keepdims=False)
    offsets = lax.dynamic_index_in_dim(rot_offset, span_at, 0, keepdims=False)
    positions = offsets[:, None] + jnp.arange(NLEN, dtype=jnp.int32)[None, :]
    key_cos, key_sin = rotary_tables(positions.reshape(NEIGH * NLEN))
    query_cos, query_sin = rotary_tables(jnp.arange(SPAN, dtype=jnp.int32))

    core = c_at.reshape(1)
    ids = jnp.stack([neighbour_ids, swapped(neighbour_ids, "c", NC)])
    copies = jnp.broadcast_to(encodings, (NX * NY, ROWS, DE))
    blocks = exchange(copies, ("x", "y"))
    asked = on_core(
        pick_kernel, "pick", jax.ShapeDtypeStruct((reads, ROWS, DE), BF16), (ids,),
        blocks, scratch=[pltpu.SemaphoreType.DMA((reads,))], space=ANY,
    )
    arrived = swapped(asked, "c", NC)

    to_z = on_core(
        spread_kernel, "spread", jax.ShapeDtypeStruct((NZ, NEIGH, ROWS, DE), BF16), (ids, core),
        blocks, arrived, scratch=[pltpu.SemaphoreType.DMA((NZ * NEIGH,))], space=ANY,
    )
    to_z, w_far = lax.optimization_barrier((to_z, w_far))
    tok = exchange(to_z, "z")
    from_pair = swapped(other, "z", NZ)
    part, dq_own, dq_pair = attention(
        tok, kv_weight, q_own, g_own, from_pair[:SPAN], from_pair[SPAN:],
        key_cos, key_sin, query_cos, query_sin, w_far,
    )

    from_heads = exchange(part, "z")
    from_heads = from_heads.reshape(NZ // spans, spans, NEIGH, ROWS, DE)
    read_sum = jnp.sum(from_heads.astype(F32), axis=0).astype(BF16).reshape(reads, ROWS, DE)

    theirs = swapped(read_sum, "c", NC)
    owners = (NX * NY, ROWS, DE)
    owner_part = on_core(
        owner_kernel, "owner_sums", jax.ShapeDtypeStruct(owners, BF16), (ids, core),
        read_sum, theirs, scratch=[pltpu.VMEM(owners, F32)],
    )
    owner_part, dq_pair = lax.optimization_barrier((owner_part, dq_pair))
    dq_back = swapped(dq_pair, "z", NZ)
    owned = jnp.sum(exchange(owner_part, ("x", "y")).astype(F32), axis=0)

    first = jnp.where(span_at == 0, dq_own, dq_back)
    second = jnp.where(span_at == 0, dq_back, dq_own)
    grad_query = jnp.concatenate([first, second], axis=0)
    return (grad_query, owned.reshape(1, ROWS, DE))


def solution(mesh):
    fine = Mesh(mesh.devices.reshape(NX, NY, NC, NZ), ("x", "y", "c", "z"))
    enc = ("x", "y", "c")
    in_specs = (
        P(enc, "z"),
        P(enc, "z"),
        P(enc, "z", None),
        P(None, None, "z"),
        P(enc, None),
        P(enc, None),
    )
    out_specs = (P(enc, "z"), P(enc, "z", None))
    return jax.shard_map(local, mesh=fine, in_specs=in_specs, out_specs=out_specs, check_vma=False)
```

```python
import math

import jax
import jax.numpy as jnp
from jax import lax
from jax.experimental import pallas as pl
from jax.experimental.pallas import tpu as pltpu
from jax.sharding import Mesh, PartitionSpec as P

HEAD = 128
DE = 896
SPAN = 64
NEIGH = 2
NLEN = 128
NX, NY, NC, NZ = 4, 8, 2, 8
ROWS = NLEN // NZ
F32, BF16 = jnp.float32, jnp.bfloat16
VMEM = pl.BlockSpec(memory_space=pltpu.VMEM)
SMEM = pl.BlockSpec(memory_space=pltpu.SMEM)
ANY = pl.BlockSpec(memory_space=pl.ANY)


def rotary_tables(positions):
    halfway = HEAD // 2
    exponent = jnp.arange(halfway, dtype=F32) * (2.0 / HEAD)
    frequency = jnp.exp(-math.log(10000.0) * exponent)
    angles = positions.astype(F32)[:, None] * frequency[None, :]
    cosine, sine = jnp.cos(angles), jnp.sin(angles)
    return jnp.concatenate([cosine, cosine], axis=-1), jnp.concatenate([-sine, sine], axis=-1)


def exchange(value, axis):
    return lax.all_to_all(value, axis, split_axis=0, concat_axis=0, tiled=True)


def shifted(value, axis, size, shift):
    return lax.ppermute(value, axis, [(i, (i + shift) % size) for i in range(size)])


def swapped(value, axis, size):
    return lax.ppermute(value, axis, [(i, i ^ 1) for i in range(size)])


def dot(a, b, over=(1, 0)):
    return lax.dot_general(
        a, b, (((over[0],), (over[1],)), ((), ())), preferred_element_type=F32
    )


def seat(block):
    return lax.div(block, NC)


def pick_kernel(ids_ref, from_ref, out_ref, sems):
    copies = []
    for read in range(out_ref.shape[0]):
        block = ids_ref[1, read // NEIGH, read % NEIGH]
        copies.append(
            pltpu.make_async_copy(from_ref.at[seat(block)], out_ref.at[read], sems.at[read])
        )
        copies[-1].start()
    for copy in copies:
        copy.wait()


def spread_kernel(ids_ref, core_ref, mine_ref, theirs_ref, out_ref, sems):
    reads = theirs_ref.shape[0]
    spans = reads // NEIGH
    places = [(read, at) for read in range(reads) for at in range(read // NEIGH, NZ, spans)]
    for count, (read, at) in enumerate(places):
        block = ids_ref[0, read // NEIGH, read % NEIGH]
        target, same = out_ref.at[at, read % NEIGH], lax.rem(block, NC) == core_ref[0]

        @pl.when(same)
        def _():
            pltpu.make_async_copy(mine_ref.at[seat(block)], target, sems.at[count]).start()

        @pl.when(jnp.logical_not(same))
        def _():
            pltpu.make_async_copy(theirs_ref.at[read], target, sems.at[count]).start()

    for count, (read, at) in enumerate(places):
        target = out_ref.at[at, read % NEIGH]
        pltpu.make_async_copy(theirs_ref.at[read], target, sems.at[count]).wait()


def near_id(near_ref, at_ref, column, read):
    return near_ref[lax.rem(at_ref[0] - column + NX, NX), read // NEIGH, read % NEIGH]


def owner_kernel(near_ref, at_ref, from_ref, mine_ref, theirs_ref, total):
    total[...] = jnp.zeros_like(total)
    here, core = at_ref[0], at_ref[1]
    for column in range(NX):
        for read in range(from_ref.shape[1]):
            block = near_id(near_ref, at_ref, column, read)

            @pl.when(block // (NY * NC) == here)
            def _():
                side = jnp.where(lax.rem(block, NC) == core, 0, NY)
                at = side + lax.rem(block // NC, NY)
                total[at] = total[at] + from_ref[column, read].astype(F32)

    mine_ref[...] = total[:NY]
    theirs_ref[...] = total[NY:].astype(BF16)


def attention_kernel(
    core_ref, tok, w_own, q_own, g_own, q_pair, g_pair, kc, ks, qc, qs, w_near, w_far,
    part, dq_own, dq_pair, dk_all, dv_all, w_pair, sems,
):
    core = core_ref[0]
    fetches = [
        pltpu.make_async_copy(w_near, w_pair.at[core], sems.at[0]),
        pltpu.make_async_copy(w_far, w_pair.at[1 - core], sems.at[1]),
    ]
    for fetch in fetches:
        fetch.start()
    scale = 1.0 / math.sqrt(HEAD)
    half = HEAD // 2
    width = w_own.shape[2]
    rows = jnp.concatenate([tok[:, n].reshape(NLEN, DE) for n in range(NEIGH)], axis=0)
    projected = [(dot(rows, w_own[0]), dot(rows, w_own[1]).astype(BF16))]
    for fetch in fetches:
        fetch.wait()
    projected.append((dot(rows, w_pair[0]), dot(rows, w_pair[1]).astype(BF16)))
    key_cos, key_sin, query_cos, query_sin = kc[...], ks[...], qc[...], qs[...]
    for turn, (q, g, dq) in enumerate(((q_own, g_own, dq_own), (q_pair, g_pair, dq_pair))):
        key_raw, values = projected[turn]
        for head in range(width // HEAD):
            cols = slice(head * HEAD, (head + 1) * HEAD)
            place = slice(turn * width + head * HEAD, turn * width + (head + 1) * HEAD)
            raw = key_raw[:, cols]
            key = (raw * key_cos + pltpu.roll(raw, half, 1) * key_sin).astype(BF16)
            value = values[:, cols]
            wide = q[:, cols].astype(F32)
            query = (wide * query_cos + pltpu.roll(wide, half, 1) * query_sin).astype(BF16)
            grad = g[:, cols]
            exponentials = jnp.exp(dot(query, key, (1, 1)) * scale)
            weights = exponentials / jnp.sum(exponentials, axis=-1, keepdims=True)
            weights_low = weights.astype(BF16)
            grad_weights = dot(grad, value, (1, 1))
            delta = jnp.sum(weights_low.astype(F32) * grad_weights, axis=-1, keepdims=True)
            grad_scores = (weights * (grad_weights - delta) * scale).astype(BF16)
            dv_all[:, place] = dot(weights_low, grad, (0, 0)).astype(BF16)
            grad_query = dot(grad_scores, key)
            dq[:, cols] = (
                grad_query * query_cos - pltpu.roll(grad_query, half, 1) * query_sin
            ).astype(BF16)
            grad_key = dot(grad_scores, query, (0, 0))
            dk_all[:, place] = (
                grad_key * key_cos - pltpu.roll(grad_key, half, 1) * key_sin
            ).astype(BF16)
    product = dot(dk_all[:, :width], w_own[0], (1, 1)) + dot(dv_all[:, :width], w_own[1], (1, 1))
    product = product + dot(dk_all[:, width:], w_pair[0], (1, 1))
    product = product + dot(dv_all[:, width:], w_pair[1], (1, 1))
    for n in range(NEIGH):
        piece = product[n * NLEN:(n + 1) * NLEN].astype(BF16)
        part[:, n] = piece.reshape(NZ, ROWS, DE)


def on_core(kernel, name, shapes, scalars, *operands, scratch=(), space=VMEM):
    return pl.pallas_call(
        kernel,
        out_shape=shapes,
        in_specs=[SMEM] * len(scalars) + [space] * len(operands),
        out_specs=jax.tree.map(lambda _: space, shapes),
        scratch_shapes=scratch,
        compiler_params=pltpu.CompilerParams(vmem_limit_bytes=16 << 20),
        name=name,
    )(*scalars, *operands)


def attention(core, *operands):
    _, depth, width = operands[1].shape
    return pl.pallas_call(
        attention_kernel,
        out_shape=(
            jax.ShapeDtypeStruct((NZ, NEIGH, ROWS, DE), BF16),
            jax.ShapeDtypeStruct((SPAN, width), BF16),
            jax.ShapeDtypeStruct((SPAN, width), BF16),
        ),
        in_specs=[SMEM] + [VMEM] * (len(operands) - 2) + [ANY] * 2,
        out_specs=(VMEM, VMEM, VMEM),
        scratch_shapes=[
            pltpu.VMEM((NEIGH * NLEN, 2 * width), BF16),
            pltpu.VMEM((NEIGH * NLEN, 2 * width), BF16),
            pltpu.VMEM((2, depth, width), BF16),
            pltpu.SemaphoreType.DMA((2,)),
        ],
        compiler_params=pltpu.CompilerParams(vmem_limit_bytes=40 << 20),
        cost_estimate=pl.CostEstimate(
            flops=2_100_000_000, bytes_accessed=6_000_000, transcendentals=131072
        ),
        name="attention",
    )(core, *operands)


def local(queries, out_grad, encodings, kv_weight, neighbour_ids, rot_offset):
    x_at, c_at, z_at = lax.axis_index("x"), lax.axis_index("c"), lax.axis_index("z")
    spans = neighbour_ids.shape[0]
    reads = spans * NEIGH
    span_at = z_at % 2

    w_near = swapped(lax.dynamic_index_in_dim(kv_weight, c_at, 0, keepdims=False), "z", NZ)
    w_far = swapped(w_near, "c", NC)
    rows_q = queries.reshape(spans, SPAN, -1)
    rows_g = out_grad.reshape(spans, SPAN, -1)
    other = jnp.concatenate(
        [
            lax.dynamic_index_in_dim(rows_q, 1 - span_at, 0, keepdims=False),
            lax.dynamic_index_in_dim(rows_g, 1 - span_at, 0, keepdims=False),
        ],
        axis=0,
    )
    from_pair = swapped(other, "z", NZ)
    q_own = lax.dynamic_index_in_dim(rows_q, span_at, 0, keepdims=False)
    g_own = lax.dynamic_index_in_dim(rows_g, span_at, 0, keepdims=False)
    offsets = lax.dynamic_index_in_dim(rot_offset, span_at, 0, keepdims=False)
    positions = offsets[:, None] + jnp.arange(NLEN, dtype=jnp.int32)[None, :]
    key_cos, key_sin = rotary_tables(positions.reshape(NEIGH * NLEN))
    query_cos, query_sin = rotary_tables(jnp.arange(SPAN, dtype=jnp.int32))

    core = c_at.reshape(1)
    at = jnp.stack([x_at, c_at])
    ids = jnp.stack([neighbour_ids, swapped(neighbour_ids, "c", NC)])
    copies = jnp.broadcast_to(encodings, (NX * NY, ROWS, DE))
    blocks = exchange(copies, ("x", "y"))
    near = [neighbour_ids] + [shifted(neighbour_ids, "x", NX, s) for s in range(1, NX)]
    blocks, near, w_far, from_pair = lax.optimization_barrier(
        (blocks, jnp.stack(near), w_far, from_pair)
    )
    asked = on_core(
        pick_kernel, "pick", jax.ShapeDtypeStruct((reads, ROWS, DE), BF16), (ids,),
        blocks, scratch=[pltpu.SemaphoreType.DMA((reads,))], space=ANY,
    )
    arrived = swapped(asked, "c", NC)

    to_z = on_core(
        spread_kernel, "spread", jax.ShapeDtypeStruct((NZ, NEIGH, ROWS, DE), BF16), (ids, core),
        blocks, arrived, scratch=[pltpu.SemaphoreType.DMA((NZ * NEIGH,))], space=ANY,
    )
    tok = exchange(to_z, "z")
    part, dq_own, dq_pair = attention(
        core, tok, kv_weight, q_own, g_own, from_pair[:SPAN], from_pair[SPAN:],
        key_cos, key_sin, query_cos, query_sin, w_near, w_far,
    )

    from_heads = exchange(part, "z")
    from_heads = from_heads.reshape(NZ // spans, spans, NEIGH, ROWS, DE)
    read_sum = jnp.sum(from_heads.astype(F32), axis=0).astype(BF16).reshape(reads, ROWS, DE)

    read_copies = jnp.broadcast_to(read_sum, (NX, reads, ROWS, DE))
    read_x = exchange(read_copies, "x")
    owners = (NY, ROWS, DE)
    mine, theirs = on_core(
        owner_kernel, "owner_sums",
        (jax.ShapeDtypeStruct(owners, F32), jax.ShapeDtypeStruct(owners, BF16)),
        (near, at), read_x, scratch=[pltpu.VMEM((NC * NY, ROWS, DE), F32)],
    )
    owner_part = (mine + swapped(theirs, "c", NC).astype(F32)).astype(BF16)
    owner_part, dq_pair = lax.optimization_barrier((owner_part, dq_pair))
    dq_back = swapped(dq_pair, "z", NZ)
    from_y = exchange(owner_part, "y")
    owned = jnp.sum(from_y.astype(F32), axis=0)

    first = jnp.where(span_at == 0, dq_own, dq_back)
    second = jnp.where(span_at == 0, dq_back, dq_own)
    grad_query = jnp.concatenate([first, second], axis=0)
    return (grad_query, owned.reshape(1, ROWS, DE))


def solution(mesh):
    fine = Mesh(mesh.devices.reshape(NX, NY, NC, NZ), ("x", "y", "c", "z"))
    enc = ("x", "y", "c")
    in_specs = (
        P(enc, "z"),
        P(enc, "z"),
        P(enc, "z", None),
        P(None, None, "z"),
        P(enc, None),
        P(enc, None),
    )
    out_specs = (P(enc, "z"), P(enc, "z", None))
    return jax.shard_map(local, mesh=fine, in_specs=in_specs, out_specs=out_specs, check_vma=False)
```

```python
import math

import jax
import jax.numpy as jnp
from jax import lax
from jax.experimental import pallas as pl
from jax.experimental.pallas import tpu as pltpu
from jax.sharding import Mesh, PartitionSpec as P

HEAD = 128
DE = 896
SPAN = 64
NEIGH = 2
NLEN = 128
NX, NY, NC, NZ = 4, 8, 2, 8
ROWS = NLEN // NZ
F32, BF16 = jnp.float32, jnp.bfloat16
VMEM = pl.BlockSpec(memory_space=pltpu.VMEM)
SMEM = pl.BlockSpec(memory_space=pltpu.SMEM)
ANY = pl.BlockSpec(memory_space=pl.ANY)


def rotary_tables(positions):
    halfway = HEAD // 2
    exponent = jnp.arange(halfway, dtype=F32) * (2.0 / HEAD)
    frequency = jnp.exp(-math.log(10000.0) * exponent)
    angles = positions.astype(F32)[:, None] * frequency[None, :]
    cosine, sine = jnp.cos(angles), jnp.sin(angles)
    return jnp.concatenate([cosine, cosine], axis=-1), jnp.concatenate([-sine, sine], axis=-1)


def shifted(value, axis, size, shift):
    return lax.ppermute(value, axis, [(i, (i + shift) % size) for i in range(size)])


def swapped(value, axis, size):
    return lax.ppermute(value, axis, [(i, i ^ 1) for i in range(size)])


def dot(a, b, over=(1, 0)):
    return lax.dot_general(
        a, b, (((over[0],), (over[1],)), ((), ())), preferred_element_type=F32
    )


def at_distance(at_ref, distance):
    return lax.rem(at_ref[0] - distance + NX, NX)


def pick_kernel(at_ref, *refs):
    near, (mine_ref, theirs_ref, out_ref, sems) = refs[:NX], refs[NX:]
    core, reads = at_ref[1], out_ref.shape[1]
    for distance in range(NX):
        column = at_distance(at_ref, distance)
        for read in range(reads):
            block = near[distance][read // NEIGH, read % NEIGH]
            row, same = lax.rem(block // NC, NY), lax.rem(block, NC) == core
            sem = sems.at[distance * reads + read]

            @pl.when(same)
            def _():
                pltpu.make_async_copy(mine_ref.at[row], out_ref.at[column, read], sem).start()

            @pl.when(jnp.logical_not(same))
            def _():
                pltpu.make_async_copy(theirs_ref.at[row], out_ref.at[column, read], sem).start()

    for count in range(NX * reads):
        place = out_ref.at[count // reads, count % reads]
        pltpu.make_async_copy(mine_ref.at[0], place, sems.at[count]).wait()


def spread_kernel(ids_ref, from_ref, out_ref):
    reads = from_ref.shape[1]
    spans = reads // NEIGH
    for read in range(reads):
        owner = ids_ref[read // NEIGH, read % NEIGH]
        block = from_ref[owner // (NY * NC), read]
        for at in range(read // NEIGH, NZ, spans):
            out_ref[at, read % NEIGH] = block


def owner_kernel(at_ref, *refs):
    near, (from_ref, mine_ref, theirs_ref, total) = refs[:NX], refs[NX:]
    total[...] = jnp.zeros_like(total)
    here, core = at_ref[0], at_ref[1]
    for distance in range(NX):
        column = at_distance(at_ref, distance)
        for read in range(from_ref.shape[1]):
            block = near[distance][read // NEIGH, read % NEIGH]

            @pl.when(block // (NY * NC) == here)
            def _():
                side = jnp.where(lax.rem(block, NC) == core, 0, NY)
                at = side + lax.rem(block // NC, NY)
                total[at] = total[at] + from_ref[column, read].astype(F32)

    mine_ref[...] = total[:NY]
    theirs_ref[...] = total[NY:].astype(BF16)


def attention_kernel(
    tok, w_own, q_own, g_own, q_pair, g_pair, kc, ks, qc, qs, w_far,
    part, dq_own, dq_pair, dk_all, dv_all, w_pair, sem,
):
    fetch = pltpu.make_async_copy(w_far, w_pair, sem)
    fetch.start()
    scale = 1.0 / math.sqrt(HEAD)
    half = HEAD // 2
    width = w_own.shape[2]
    rows = jnp.concatenate([tok[:, n].reshape(NLEN, DE) for n in range(NEIGH)], axis=0)
    projected = [(dot(rows, w_own[0]), dot(rows, w_own[1]).astype(BF16))]
    fetch.wait()
    projected.append((dot(rows, w_pair[0]), dot(rows, w_pair[1]).astype(BF16)))
    key_cos, key_sin, query_cos, query_sin = kc[...], ks[...], qc[...], qs[...]
    for turn, (q, g, dq) in enumerate(((q_own, g_own, dq_own), (q_pair, g_pair, dq_pair))):
        key_raw, values = projected[turn]
        for head in range(width // HEAD):
            cols = slice(head * HEAD, (head + 1) * HEAD)
            place = slice(turn * width + head * HEAD, turn * width + (head + 1) * HEAD)
            raw = key_raw[:, cols]
            key = (raw * key_cos + pltpu.roll(raw, half, 1) * key_sin).astype(BF16)
            value = values[:, cols]
            wide = q[:, cols].astype(F32)
            query = (wide * query_cos + pltpu.roll(wide, half, 1) * query_sin).astype(BF16)
            grad = g[:, cols]
            exponentials = jnp.exp(dot(query, key, (1, 1)) * scale)
            weights = exponentials / jnp.sum(exponentials, axis=-1, keepdims=True)
            weights_low = weights.astype(BF16)
            grad_weights = dot(grad, value, (1, 1))
            delta = jnp.sum(weights_low.astype(F32) * grad_weights, axis=-1, keepdims=True)
            grad_scores = (weights * (grad_weights - delta) * scale).astype(BF16)
            dv_all[:, place] = dot(weights_low, grad, (0, 0)).astype(BF16)
            grad_query = dot(grad_scores, key)
            dq[:, cols] = (
                grad_query * query_cos - pltpu.roll(grad_query, half, 1) * query_sin
            ).astype(BF16)
            grad_key = dot(grad_scores, query, (0, 0))
            dk_all[:, place] = (
                grad_key * key_cos - pltpu.roll(grad_key, half, 1) * key_sin
            ).astype(BF16)
    product = dot(dk_all[:, :width], w_own[0], (1, 1)) + dot(dv_all[:, :width], w_own[1], (1, 1))
    product = product + dot(dk_all[:, width:], w_pair[0], (1, 1))
    product = product + dot(dv_all[:, width:], w_pair[1], (1, 1))
    for n in range(NEIGH):
        piece = product[n * NLEN:(n + 1) * NLEN].astype(BF16)
        part[:, n] = piece.reshape(NZ, ROWS, DE)


def on_core(kernel, name, shapes, scalars, *operands, scratch=(), space=VMEM):
    return pl.pallas_call(
        kernel,
        out_shape=shapes,
        in_specs=[SMEM] * len(scalars) + [space] * len(operands),
        out_specs=jax.tree.map(lambda _: space, shapes),
        scratch_shapes=scratch,
        compiler_params=pltpu.CompilerParams(vmem_limit_bytes=16 << 20),
        name=name,
    )(*scalars, *operands)


def attention(*operands):
    _, depth, width = operands[1].shape
    return pl.pallas_call(
        attention_kernel,
        out_shape=(
            jax.ShapeDtypeStruct((NZ, NEIGH, ROWS, DE), BF16),
            jax.ShapeDtypeStruct((SPAN, width), BF16),
            jax.ShapeDtypeStruct((SPAN, width), BF16),
        ),
        in_specs=[VMEM] * (len(operands) - 1) + [ANY],
        out_specs=(VMEM, VMEM, VMEM),
        scratch_shapes=[
            pltpu.VMEM((NEIGH * NLEN, 2 * width), BF16),
            pltpu.VMEM((NEIGH * NLEN, 2 * width), BF16),
            pltpu.VMEM((2, depth, width), BF16),
            pltpu.SemaphoreType.DMA,
        ],
        compiler_params=pltpu.CompilerParams(vmem_limit_bytes=40 << 20),
        cost_estimate=pl.CostEstimate(
            flops=2_100_000_000, bytes_accessed=6_000_000, transcendentals=131072
        ),
        name="attention",
    )(*operands)


def local(queries, out_grad, encodings, kv_weight, neighbour_ids, rot_offset):
    x_at, c_at, z_at = lax.axis_index("x"), lax.axis_index("c"), lax.axis_index("z")
    spans = neighbour_ids.shape[0]
    reads = spans * NEIGH
    span_at = z_at % 2

    w_far = swapped(kv_weight, "z", NZ)
    rows_q = queries.reshape(spans, SPAN, -1)
    rows_g = out_grad.reshape(spans, SPAN, -1)
    other = jnp.concatenate(
        [
            lax.dynamic_index_in_dim(rows_q, 1 - span_at, 0, keepdims=False),
            lax.dynamic_index_in_dim(rows_g, 1 - span_at, 0, keepdims=False),
        ],
        axis=0,
    )
    q_own = lax.dynamic_index_in_dim(rows_q, span_at, 0, keepdims=False)
    g_own = lax.dynamic_index_in_dim(rows_g, span_at, 0, keepdims=False)
    offsets = lax.dynamic_index_in_dim(rot_offset, span_at, 0, keepdims=False)
    positions = offsets[:, None] + jnp.arange(NLEN, dtype=jnp.int32)[None, :]
    key_cos, key_sin = rotary_tables(positions.reshape(NEIGH * NLEN))
    query_cos, query_sin = rotary_tables(jnp.arange(SPAN, dtype=jnp.int32))

    at = jnp.stack([x_at, c_at])
    near = [neighbour_ids] + [shifted(neighbour_ids, "x", NX, s) for s in range(1, NX)]
    copies = jnp.broadcast_to(encodings, (NY, ROWS, DE))
    over_y = lax.all_to_all(copies, "y", split_axis=0, concat_axis=0, tiled=True)
    over_y, near, other = lax.optimization_barrier((over_y, near, other))
    beside = swapped(over_y, "c", NC)
    block = (reads, ROWS, DE)
    asked = on_core(
        pick_kernel, "pick", jax.ShapeDtypeStruct((NX, *block), BF16), (at, *near),
        over_y, beside, scratch=[pltpu.SemaphoreType.DMA((NX * reads,))], space=ANY,
    )
    found = lax.all_to_all(asked, "x", split_axis=0, concat_axis=0, tiled=True)

    to_z = on_core(
        spread_kernel, "spread", jax.ShapeDtypeStruct((NZ, NEIGH, ROWS, DE), BF16), (neighbour_ids,),
        found,
    )
    from_pair = swapped(other, "z", NZ)
    to_z, w_far, from_pair = lax.optimization_barrier((to_z, w_far, from_pair))
    tok = lax.all_to_all(to_z, "z", split_axis=0, concat_axis=0, tiled=True)
    part, dq_own, dq_pair = attention(
        tok, kv_weight, q_own, g_own, from_pair[:SPAN], from_pair[SPAN:],
        key_cos, key_sin, query_cos, query_sin, w_far,
    )

    from_heads = lax.all_to_all(part, "z", split_axis=0, concat_axis=0, tiled=True)
    from_heads = from_heads.reshape(NZ // spans, spans, NEIGH, ROWS, DE)
    read_sum = jnp.sum(from_heads.astype(F32), axis=0).astype(BF16).reshape(reads, ROWS, DE)

    read_copies = jnp.broadcast_to(read_sum, (NX, *block))
    read_x = lax.all_to_all(read_copies, "x", split_axis=0, concat_axis=0, tiled=True)
    owners = (NY, ROWS, DE)
    mine, theirs = on_core(
        owner_kernel, "owner_sums",
        (jax.ShapeDtypeStruct(owners, F32), jax.ShapeDtypeStruct(owners, BF16)),
        (at, *near), read_x, scratch=[pltpu.VMEM((NC * NY, ROWS, DE), F32)],
    )
    owner_part = (mine + swapped(theirs, "c", NC).astype(F32)).astype(BF16)
    owner_part, dq_pair = lax.optimization_barrier((owner_part, dq_pair))
    dq_back = swapped(dq_pair, "z", NZ)
    from_y = lax.all_to_all(owner_part, "y", split_axis=0, concat_axis=0, tiled=True)
    owned = jnp.sum(from_y.astype(F32), axis=0)

    first = jnp.where(span_at == 0, dq_own, dq_back)
    second = jnp.where(span_at == 0, dq_back, dq_own)
    grad_query = jnp.concatenate([first, second], axis=0)
    return (grad_query, owned.reshape(1, ROWS, DE))


def solution(mesh):
    fine = Mesh(mesh.devices.reshape(NX, NY, NC, NZ), ("x", "y", "c", "z"))
    enc = ("x", "y", "c")
    in_specs = (
        P(enc, "z"),
        P(enc, "z"),
        P(enc, "z", None),
        P(None, None, "z"),
        P(enc, None),
        P(enc, None),
    )
    out_specs = (P(enc, "z"), P(enc, "z", None))
    return jax.shard_map(local, mesh=fine, in_specs=in_specs, out_specs=out_specs, check_vma=False)
```

```python
import math

import jax
import jax.numpy as jnp
from jax import lax
from jax.experimental import pallas as pl
from jax.experimental.pallas import tpu as pltpu
from jax.sharding import Mesh, PartitionSpec as P

HEAD = 128
DE = 896
SPAN = 64
NEIGH = 2
NLEN = 128
NX, NY, NC, NZ = 4, 8, 2, 8
ROWS = NLEN // NZ
F32, BF16 = jnp.float32, jnp.bfloat16
VMEM = pl.BlockSpec(memory_space=pltpu.VMEM)
SMEM = pl.BlockSpec(memory_space=pltpu.SMEM)
ANY = pl.BlockSpec(memory_space=pl.ANY)


def rotary_tables(positions):
    halfway = HEAD // 2
    exponent = jnp.arange(halfway, dtype=F32) * (2.0 / HEAD)
    frequency = jnp.exp(-math.log(10000.0) * exponent)
    angles = positions.astype(F32)[:, None] * frequency[None, :]
    cosine, sine = jnp.cos(angles), jnp.sin(angles)
    return jnp.concatenate([cosine, cosine], axis=-1), jnp.concatenate([-sine, sine], axis=-1)


def shifted(value, axis, size, shift):
    return lax.ppermute(value, axis, [(i, (i + shift) % size) for i in range(size)])


def swapped(value, axis, size):
    return lax.ppermute(value, axis, [(i, i ^ 1) for i in range(size)])


def dot(a, b, over=(1, 0)):
    return lax.dot_general(
        a, b, (((over[0],), (over[1],)), ((), ())), preferred_element_type=F32
    )


def at_distance(at_ref, distance):
    return lax.rem(at_ref[0] - distance + NX, NX)


def copies_kernel(from_ref, out_ref, sems):
    copies = [
        pltpu.make_async_copy(from_ref.at[0], out_ref.at[at], sems.at[at])
        for at in range(out_ref.shape[0])
    ]
    for copy in copies:
        copy.start()
    for copy in copies:
        copy.wait()


def pick_kernel(at_ref, *refs):
    near, (mine_ref, theirs_ref, out_ref, sems) = refs[:NX], refs[NX:]
    core, reads = at_ref[1], out_ref.shape[1]
    for distance in range(NX):
        column = at_distance(at_ref, distance)
        for read in range(reads):
            block = near[distance][read // NEIGH, read % NEIGH]
            row, same = lax.rem(block // NC, NY), lax.rem(block, NC) == core
            sem = sems.at[distance * reads + read]

            @pl.when(same)
            def _():
                pltpu.make_async_copy(mine_ref.at[row], out_ref.at[column, read], sem).start()

            @pl.when(jnp.logical_not(same))
            def _():
                pltpu.make_async_copy(theirs_ref.at[row], out_ref.at[column, read], sem).start()

    for count in range(NX * reads):
        place = out_ref.at[count // reads, count % reads]
        pltpu.make_async_copy(mine_ref.at[0], place, sems.at[count]).wait()


def spread_kernel(ids_ref, from_ref, out_ref):
    reads = from_ref.shape[1]
    spans = reads // NEIGH
    for read in range(reads):
        owner = ids_ref[read // NEIGH, read % NEIGH]
        block = from_ref[owner // (NY * NC), read]
        for at in range(read // NEIGH, NZ, spans):
            out_ref[at, read % NEIGH] = block


def owner_kernel(at_ref, *refs):
    near, (from_ref, mine_ref, theirs_ref, total) = refs[:NX], refs[NX:]
    total[...] = jnp.zeros_like(total)
    here, core = at_ref[0], at_ref[1]
    for distance in range(NX):
        column = at_distance(at_ref, distance)
        for read in range(from_ref.shape[1]):
            block = near[distance][read // NEIGH, read % NEIGH]

            @pl.when(block // (NY * NC) == here)
            def _():
                side = jnp.where(lax.rem(block, NC) == core, 0, NY)
                at = side + lax.rem(block // NC, NY)
                total[at] = total[at] + from_ref[column, read].astype(F32)

    mine_ref[...] = total[:NY]
    theirs_ref[...] = total[NY:].astype(BF16)


def attention_kernel(
    tok, w_own, q_own, g_own, q_pair, g_pair, kc, ks, qc, qs, w_pair,
    part, dq_own, dq_pair, dk_all, dv_all,
):
    scale = 1.0 / math.sqrt(HEAD)
    half = HEAD // 2
    width = w_own.shape[2]
    rows = jnp.concatenate([tok[:, n].reshape(NLEN, DE) for n in range(NEIGH)], axis=0)
    projected = [(dot(rows, w_own[0]), dot(rows, w_own[1]).astype(BF16))]
    projected.append((dot(rows, w_pair[0]), dot(rows, w_pair[1]).astype(BF16)))
    key_cos, key_sin, query_cos, query_sin = kc[...], ks[...], qc[...], qs[...]
    for turn, (q, g, dq) in enumerate(((q_own, g_own, dq_own), (q_pair, g_pair, dq_pair))):
        key_raw, values = projected[turn]
        for head in range(width // HEAD):
            cols = slice(head * HEAD, (head + 1) * HEAD)
            place = slice(turn * width + head * HEAD, turn * width + (head + 1) * HEAD)
            raw = key_raw[:, cols]
            key = (raw * key_cos + pltpu.roll(raw, half, 1) * key_sin).astype(BF16)
            value = values[:, cols]
            wide = q[:, cols].astype(F32)
            query = (wide * query_cos + pltpu.roll(wide, half, 1) * query_sin).astype(BF16)
            grad = g[:, cols]
            exponentials = jnp.exp(dot(query, key, (1, 1)) * scale)
            weights = exponentials / jnp.sum(exponentials, axis=-1, keepdims=True)
            weights_low = weights.astype(BF16)
            grad_weights = dot(grad, value, (1, 1))
            delta = jnp.sum(weights_low.astype(F32) * grad_weights, axis=-1, keepdims=True)
            grad_scores = (weights * (grad_weights - delta) * scale).astype(BF16)
            dv_all[:, place] = dot(weights_low, grad, (0, 0)).astype(BF16)
            grad_query = dot(grad_scores, key)
            dq[:, cols] = (
                grad_query * query_cos - pltpu.roll(grad_query, half, 1) * query_sin
            ).astype(BF16)
            grad_key = dot(grad_scores, query, (0, 0))
            dk_all[:, place] = (
                grad_key * key_cos - pltpu.roll(grad_key, half, 1) * key_sin
            ).astype(BF16)
    product = dot(dk_all[:, :width], w_own[0], (1, 1)) + dot(dv_all[:, :width], w_own[1], (1, 1))
    product = product + dot(dk_all[:, width:], w_pair[0], (1, 1))
    product = product + dot(dv_all[:, width:], w_pair[1], (1, 1))
    for n in range(NEIGH):
        piece = product[n * NLEN:(n + 1) * NLEN].astype(BF16)
        part[:, n] = piece.reshape(NZ, ROWS, DE)


def on_core(kernel, name, shapes, scalars, *operands, scratch=(), space=VMEM):
    return pl.pallas_call(
        kernel,
        out_shape=shapes,
        in_specs=[SMEM] * len(scalars) + [space] * len(operands),
        out_specs=jax.tree.map(lambda _: space, shapes),
        scratch_shapes=scratch,
        compiler_params=pltpu.CompilerParams(vmem_limit_bytes=16 << 20),
        name=name,
    )(*scalars, *operands)


def attention(*operands):
    width = operands[1].shape[2]
    return pl.pallas_call(
        attention_kernel,
        out_shape=(
            jax.ShapeDtypeStruct((NZ, NEIGH, ROWS, DE), BF16),
            jax.ShapeDtypeStruct((SPAN, width), BF16),
            jax.ShapeDtypeStruct((SPAN, width), BF16),
        ),
        in_specs=[VMEM] * len(operands),
        out_specs=(VMEM, VMEM, VMEM),
        scratch_shapes=[
            pltpu.VMEM((NEIGH * NLEN, 2 * width), BF16),
            pltpu.VMEM((NEIGH * NLEN, 2 * width), BF16),
        ],
        compiler_params=pltpu.CompilerParams(vmem_limit_bytes=40 << 20),
        cost_estimate=pl.CostEstimate(
            flops=2_100_000_000, bytes_accessed=6_000_000, transcendentals=131072
        ),
        name="attention",
    )(*operands)


def local(queries, out_grad, encodings, kv_weight, neighbour_ids, rot_offset):
    x_at, c_at, z_at = lax.axis_index("x"), lax.axis_index("c"), lax.axis_index("z")
    spans = neighbour_ids.shape[0]
    reads = spans * NEIGH
    span_at = z_at % 2

    w_far = swapped(kv_weight, "z", NZ)
    rows_q = queries.reshape(spans, SPAN, -1)
    rows_g = out_grad.reshape(spans, SPAN, -1)
    other = jnp.concatenate(
        [
            lax.dynamic_index_in_dim(rows_q, 1 - span_at, 0, keepdims=False),
            lax.dynamic_index_in_dim(rows_g, 1 - span_at, 0, keepdims=False),
        ],
        axis=0,
    )
    q_own = lax.dynamic_index_in_dim(rows_q, span_at, 0, keepdims=False)
    g_own = lax.dynamic_index_in_dim(rows_g, span_at, 0, keepdims=False)
    offsets = lax.dynamic_index_in_dim(rot_offset, span_at, 0, keepdims=False)
    positions = offsets[:, None] + jnp.arange(NLEN, dtype=jnp.int32)[None, :]
    key_cos, key_sin = rotary_tables(positions.reshape(NEIGH * NLEN))
    query_cos, query_sin = rotary_tables(jnp.arange(SPAN, dtype=jnp.int32))

    at = jnp.stack([x_at, c_at])
    ids = jnp.maximum(neighbour_ids, 0)
    near = [ids] + [shifted(neighbour_ids, "x", NX, s) for s in range(1, NX)]
    copies = on_core(
        copies_kernel, "copies", jax.ShapeDtypeStruct((NY, ROWS, DE), BF16), (),
        encodings, scratch=[pltpu.SemaphoreType.DMA((NY,))], space=ANY,
    )
    over_y = lax.all_to_all(copies, "y", split_axis=0, concat_axis=0, tiled=True)
    over_y, near, other = lax.optimization_barrier((over_y, near, other))
    beside = swapped(over_y, "c", NC)
    block = (reads, ROWS, DE)
    asked = on_core(
        pick_kernel, "pick", jax.ShapeDtypeStruct((NX, *block), BF16), (at, *near),
        over_y, beside, scratch=[pltpu.SemaphoreType.DMA((NX * reads,))], space=ANY,
    )
    found = lax.all_to_all(asked, "x", split_axis=0, concat_axis=0, tiled=True)

    to_z = on_core(
        spread_kernel, "spread", jax.ShapeDtypeStruct((NZ, NEIGH, ROWS, DE), BF16), (near[0],),
        found,
    )
    from_pair = swapped(other, "z", NZ)
    to_z, w_far, from_pair = lax.optimization_barrier((to_z, w_far, from_pair))
    tok = lax.all_to_all(to_z, "z", split_axis=0, concat_axis=0, tiled=True)
    part, dq_own, dq_pair = attention(
        tok, kv_weight, q_own, g_own, from_pair[:SPAN], from_pair[SPAN:],
        key_cos, key_sin, query_cos, query_sin, w_far,
    )

    from_heads = lax.all_to_all(part, "z", split_axis=0, concat_axis=0, tiled=True)
    from_heads = from_heads.reshape(NZ // spans, spans, NEIGH, ROWS, DE)
    read_sum = jnp.sum(from_heads.astype(F32), axis=0).astype(BF16).reshape(reads, ROWS, DE)

    read_copies = jnp.broadcast_to(read_sum, (NX, *block))
    read_copies, dq_pair = lax.optimization_barrier((read_copies, dq_pair))
    read_x = lax.all_to_all(read_copies, "x", split_axis=0, concat_axis=0, tiled=True)
    dq_back = swapped(dq_pair, "z", NZ)
    read_x, dq_back = lax.optimization_barrier((read_x, dq_back))
    owners = (NY, ROWS, DE)
    mine, theirs = on_core(
        owner_kernel, "owner_sums",
        (jax.ShapeDtypeStruct(owners, F32), jax.ShapeDtypeStruct(owners, BF16)),
        (at, *near), read_x, scratch=[pltpu.VMEM((NC * NY, ROWS, DE), F32)],
    )
    owner_part = (mine + swapped(theirs, "c", NC).astype(F32)).astype(BF16)
    from_y = lax.all_to_all(owner_part, "y", split_axis=0, concat_axis=0, tiled=True)
    owned = jnp.sum(from_y.astype(F32), axis=0)

    first = jnp.where(span_at == 0, dq_own, dq_back)
    second = jnp.where(span_at == 0, dq_back, dq_own)
    grad_query = jnp.concatenate([first, second], axis=0)
    return (grad_query, owned.reshape(1, ROWS, DE))


def solution(mesh):
    fine = Mesh(mesh.devices.reshape(NX, NY, NC, NZ), ("x", "y", "c", "z"))
    enc = ("x", "y", "c")
    in_specs = (
        P(enc, "z"),
        P(enc, "z"),
        P(enc, "z", None),
        P(None, None, "z"),
        P(enc, None),
        P(enc, None),
    )
    out_specs = (P(enc, "z"), P(enc, "z", None))
    return jax.shard_map(local, mesh=fine, in_specs=in_specs, out_specs=out_specs, check_vma=False)
```

```python
import math

import jax
import jax.numpy as jnp
from jax import lax
from jax.experimental import pallas as pl
from jax.experimental.pallas import tpu as pltpu
from jax.sharding import Mesh, PartitionSpec as P

HEAD = 128
DE = 896
SPAN = 64
NEIGH = 2
NLEN = 128
NX, NY, NC, NZ = 4, 8, 2, 8
ROWS = NLEN // NZ
F32, BF16 = jnp.float32, jnp.bfloat16
VMEM = pl.BlockSpec(memory_space=pltpu.VMEM)
SMEM = pl.BlockSpec(memory_space=pltpu.SMEM)
ANY = pl.BlockSpec(memory_space=pl.ANY)


def rotary_tables(positions):
    halfway = HEAD // 2
    exponent = jnp.arange(halfway, dtype=F32) * (2.0 / HEAD)
    frequency = jnp.exp(-math.log(10000.0) * exponent)
    angles = positions.astype(F32)[:, None] * frequency[None, :]
    cosine, sine = jnp.cos(angles), jnp.sin(angles)
    return jnp.concatenate([cosine, cosine], axis=-1), jnp.concatenate([-sine, sine], axis=-1)


def shifted(value, axis, size, shift):
    return lax.ppermute(value, axis, [(i, (i + shift) % size) for i in range(size)])


def swapped(value, axis, size):
    return lax.ppermute(value, axis, [(i, i ^ 1) for i in range(size)])


def dot(a, b, over=(1, 0)):
    return lax.dot_general(
        a, b, (((over[0],), (over[1],)), ((), ())), preferred_element_type=F32
    )


def at_distance(at_ref, distance):
    return lax.rem(at_ref[0] - distance + NX, NX)


def pick_kernel(at_ref, *refs):
    near, (mine_ref, theirs_ref, out_ref, sems) = refs[:NX], refs[NX:]
    core, reads = at_ref[1], out_ref.shape[1]
    for distance in range(NX):
        column = at_distance(at_ref, distance)
        for read in range(reads):
            block = near[distance][read // NEIGH, read % NEIGH]
            row, same = lax.rem(block // NC, NY), lax.rem(block, NC) == core
            sem = sems.at[distance * reads + read]

            @pl.when(same)
            def _():
                pltpu.make_async_copy(mine_ref.at[row], out_ref.at[column, read], sem).start()

            @pl.when(jnp.logical_not(same))
            def _():
                pltpu.make_async_copy(theirs_ref.at[row], out_ref.at[column, read], sem).start()

    for count in range(NX * reads):
        place = out_ref.at[count // reads, count % reads]
        pltpu.make_async_copy(mine_ref.at[0], place, sems.at[count]).wait()


def spread_kernel(ids_ref, from_ref, out_ref):
    reads = from_ref.shape[1]
    spans = reads // NEIGH
    for read in range(reads):
        owner = ids_ref[read // NEIGH, read % NEIGH]
        block = from_ref[owner // (NY * NC), read]
        for at in range(read // NEIGH, NZ, spans):
            out_ref[at, read % NEIGH] = block


def owner_kernel(at_ref, *refs):
    near, (from_ref, mine_ref, theirs_ref, total) = refs[:NX], refs[NX:]
    total[...] = jnp.zeros_like(total)
    here, core = at_ref[0], at_ref[1]
    for distance in range(NX):
        column = at_distance(at_ref, distance)
        for read in range(from_ref.shape[1]):
            block = near[distance][read // NEIGH, read % NEIGH]

            @pl.when(block // (NY * NC) == here)
            def _():
                side = jnp.where(lax.rem(block, NC) == core, 0, NY)
                at = side + lax.rem(block // NC, NY)
                total[at] = total[at] + from_ref[column, read].astype(F32)

    mine_ref[...] = total[:NY]
    theirs_ref[...] = total[NY:].astype(BF16)


def attention_kernel(
    tok, w_own, q_own, g_own, q_pair, g_pair, kc, ks, qc, qs, w_far,
    part, dq_own, dq_pair, dk_all, dv_all, w_pair, sem,
):
    fetch = pltpu.make_async_copy(w_far, w_pair, sem)
    fetch.start()
    scale = 1.0 / math.sqrt(HEAD)
    half = HEAD // 2
    width = w_own.shape[2]
    rows = jnp.concatenate([tok[:, n].reshape(NLEN, DE) for n in range(NEIGH)], axis=0)
    projected = [(dot(rows, w_own[0]), dot(rows, w_own[1]).astype(BF16))]
    fetch.wait()
    projected.append((dot(rows, w_pair[0]), dot(rows, w_pair[1]).astype(BF16)))
    key_cos, key_sin, query_cos, query_sin = kc[...], ks[...], qc[...], qs[...]
    for turn, (q, g, dq) in enumerate(((q_own, g_own, dq_own), (q_pair, g_pair, dq_pair))):
        key_raw, values = projected[turn]
        for head in range(width // HEAD):
            cols = slice(head * HEAD, (head + 1) * HEAD)
            place = slice(turn * width + head * HEAD, turn * width + (head + 1) * HEAD)
            raw = key_raw[:, cols]
            key = (raw * key_cos + pltpu.roll(raw, half, 1) * key_sin).astype(BF16)
            value = values[:, cols]
            wide = q[:, cols].astype(F32)
            query = (wide * query_cos + pltpu.roll(wide, half, 1) * query_sin).astype(BF16)
            grad = g[:, cols]
            exponentials = jnp.exp(dot(query, key, (1, 1)) * scale)
            weights = exponentials / jnp.sum(exponentials, axis=-1, keepdims=True)
            weights_low = weights.astype(BF16)
            grad_weights = dot(grad, value, (1, 1))
            delta = jnp.sum(weights_low.astype(F32) * grad_weights, axis=-1, keepdims=True)
            grad_scores = (weights * (grad_weights - delta) * scale).astype(BF16)
            dv_all[:, place] = dot(weights_low, grad, (0, 0)).astype(BF16)
            grad_query = dot(grad_scores, key)
            dq[:, cols] = (
                grad_query * query_cos - pltpu.roll(grad_query, half, 1) * query_sin
            ).astype(BF16)
            grad_key = dot(grad_scores, query, (0, 0))
            dk_all[:, place] = (
                grad_key * key_cos - pltpu.roll(grad_key, half, 1) * key_sin
            ).astype(BF16)
    product = dot(dk_all[:, :width], w_own[0], (1, 1)) + dot(dv_all[:, :width], w_own[1], (1, 1))
    product = product + dot(dk_all[:, width:], w_pair[0], (1, 1))
    product = product + dot(dv_all[:, width:], w_pair[1], (1, 1))
    for n in range(NEIGH):
        piece = product[n * NLEN:(n + 1) * NLEN].astype(BF16)
        part[:, n] = piece.reshape(NZ, ROWS, DE)


def on_core(kernel, name, shapes, scalars, *operands, scratch=(), space=VMEM):
    return pl.pallas_call(
        kernel,
        out_shape=shapes,
        in_specs=[SMEM] * len(scalars) + [space] * len(operands),
        out_specs=jax.tree.map(lambda _: space, shapes),
        scratch_shapes=scratch,
        compiler_params=pltpu.CompilerParams(vmem_limit_bytes=16 << 20),
        name=name,
    )(*scalars, *operands)


def attention(*operands):
    _, depth, width = operands[1].shape
    return pl.pallas_call(
        attention_kernel,
        out_shape=(
            jax.ShapeDtypeStruct((NZ, NEIGH, ROWS, DE), BF16),
            jax.ShapeDtypeStruct((SPAN, width), BF16),
            jax.ShapeDtypeStruct((SPAN, width), BF16),
        ),
        in_specs=[VMEM] * (len(operands) - 1) + [ANY],
        out_specs=(VMEM, VMEM, VMEM),
        scratch_shapes=[
            pltpu.VMEM((NEIGH * NLEN, 2 * width), BF16),
            pltpu.VMEM((NEIGH * NLEN, 2 * width), BF16),
            pltpu.VMEM((2, depth, width), BF16),
            pltpu.SemaphoreType.DMA,
        ],
        compiler_params=pltpu.CompilerParams(vmem_limit_bytes=40 << 20),
        cost_estimate=pl.CostEstimate(
            flops=2_100_000_000, bytes_accessed=6_000_000, transcendentals=131072
        ),
        name="attention",
    )(*operands)


def local(queries, out_grad, encodings, kv_weight, neighbour_ids, rot_offset):
    x_at, c_at, z_at = lax.axis_index("x"), lax.axis_index("c"), lax.axis_index("z")
    spans = neighbour_ids.shape[0]
    reads = spans * NEIGH
    span_at = z_at % 2

    w_far = swapped(kv_weight, "z", NZ)
    rows_q = queries.reshape(spans, SPAN, -1)
    rows_g = out_grad.reshape(spans, SPAN, -1)
    other = jnp.concatenate(
        [
            lax.dynamic_index_in_dim(rows_q, 1 - span_at, 0, keepdims=False),
            lax.dynamic_index_in_dim(rows_g, 1 - span_at, 0, keepdims=False),
        ],
        axis=0,
    )
    q_own = lax.dynamic_index_in_dim(rows_q, span_at, 0, keepdims=False)
    g_own = lax.dynamic_index_in_dim(rows_g, span_at, 0, keepdims=False)
    offsets = lax.dynamic_index_in_dim(rot_offset, span_at, 0, keepdims=False)
    positions = offsets[:, None] + jnp.arange(NLEN, dtype=jnp.int32)[None, :]
    key_cos, key_sin = rotary_tables(positions.reshape(NEIGH * NLEN))
    query_cos, query_sin = rotary_tables(jnp.arange(SPAN, dtype=jnp.int32))

    at = jnp.stack([x_at, c_at])
    near = [neighbour_ids] + [shifted(neighbour_ids, "x", NX, s) for s in range(1, NX)]
    copies = jnp.broadcast_to(encodings, (NY, ROWS, DE))
    over_y = lax.all_to_all(copies, "y", split_axis=0, concat_axis=0, tiled=True)
    over_y, near, other = lax.optimization_barrier((over_y, near, other))
    beside = swapped(over_y, "c", NC)
    block = (reads, ROWS, DE)
    asked = on_core(
        pick_kernel, "pick", jax.ShapeDtypeStruct((NX, *block), BF16), (at, *near),
        over_y, beside, scratch=[pltpu.SemaphoreType.DMA((NX * reads,))], space=ANY,
    )
    found = lax.all_to_all(asked, "x", split_axis=0, concat_axis=0, tiled=True)

    to_z = on_core(
        spread_kernel, "spread", jax.ShapeDtypeStruct((NZ, NEIGH, ROWS, DE), BF16), (neighbour_ids,),
        found,
    )
    from_pair = swapped(other, "z", NZ)
    to_z, w_far, from_pair = lax.optimization_barrier((to_z, w_far, from_pair))
    tok = lax.all_to_all(to_z, "z", split_axis=0, concat_axis=0, tiled=True)
    part, dq_own, dq_pair = attention(
        tok, kv_weight, q_own, g_own, from_pair[:SPAN], from_pair[SPAN:],
        key_cos, key_sin, query_cos, query_sin, w_far,
    )

    from_heads = lax.all_to_all(part, "z", split_axis=0, concat_axis=0, tiled=True)
    from_heads = from_heads.reshape(NZ // spans, spans, NEIGH, ROWS, DE)
    read_sum = jnp.sum(from_heads.astype(F32), axis=0).astype(BF16).reshape(reads, ROWS, DE)

    read_copies = jnp.broadcast_to(read_sum, (NX, *block))
    read_copies, dq_pair = lax.optimization_barrier((read_copies, dq_pair))
    read_x = lax.all_to_all(read_copies, "x", split_axis=0, concat_axis=0, tiled=True)
    dq_back = swapped(dq_pair, "z", NZ)
    read_x, dq_back = lax.optimization_barrier((read_x, dq_back))
    owners = (NY, ROWS, DE)
    mine, theirs = on_core(
        owner_kernel, "owner_sums",
        (jax.ShapeDtypeStruct(owners, F32), jax.ShapeDtypeStruct(owners, BF16)),
        (at, *near), read_x, scratch=[pltpu.VMEM((NC * NY, ROWS, DE), F32)],
    )
    owner_part = (mine + swapped(theirs, "c", NC).astype(F32)).astype(BF16)
    from_y = lax.all_to_all(owner_part, "y", split_axis=0, concat_axis=0, tiled=True)
    owned = jnp.sum(from_y.astype(F32), axis=0)

    first = jnp.where(span_at == 0, dq_own, dq_back)
    second = jnp.where(span_at == 0, dq_back, dq_own)
    grad_query = jnp.concatenate([first, second], axis=0)
    return (grad_query, owned.reshape(1, ROWS, DE))


def solution(mesh):
    fine = Mesh(mesh.devices.reshape(NX, NY, NC, NZ), ("x", "y", "c", "z"))
    enc = ("x", "y", "c")
    in_specs = (
        P(enc, "z"),
        P(enc, "z"),
        P(enc, "z", None),
        P(None, None, "z"),
        P(enc, None),
        P(enc, None),
    )
    out_specs = (P(enc, "z"), P(enc, "z", None))
    return jax.shard_map(local, mesh=fine, in_specs=in_specs, out_specs=out_specs, check_vma=False)
```

```python
import math

import jax
import jax.numpy as jnp
from jax import lax
from jax.experimental import pallas as pl
from jax.experimental.pallas import tpu as pltpu
from jax.sharding import Mesh, PartitionSpec as P

HEAD = 128
DE = 896
SPAN = 64
NEIGH = 2
NLEN = 128
NX, NY, NC, NZ = 4, 8, 2, 8
ROWS = NLEN // NZ
F32, BF16 = jnp.float32, jnp.bfloat16
VMEM = pl.BlockSpec(memory_space=pltpu.VMEM)
SMEM = pl.BlockSpec(memory_space=pltpu.SMEM)
ANY = pl.BlockSpec(memory_space=pl.ANY)


def rotary_tables(positions):
    halfway = HEAD // 2
    exponent = jnp.arange(halfway, dtype=F32) * (2.0 / HEAD)
    frequency = jnp.exp(-math.log(10000.0) * exponent)
    angles = positions.astype(F32)[:, None] * frequency[None, :]
    cosine, sine = jnp.cos(angles), jnp.sin(angles)
    return jnp.concatenate([cosine, cosine], axis=-1), jnp.concatenate([-sine, sine], axis=-1)


def shifted(value, axis, size, shift):
    return lax.ppermute(value, axis, [(i, (i + shift) % size) for i in range(size)])


def swapped(value, axis, size):
    return lax.ppermute(value, axis, [(i, i ^ 1) for i in range(size)])


def dot(a, b, over=(1, 0)):
    return lax.dot_general(
        a, b, (((over[0],), (over[1],)), ((), ())), preferred_element_type=F32
    )


def at_distance(at_ref, distance):
    return lax.rem(at_ref[0] - distance + NX, NX)


def pick_kernel(at_ref, *refs):
    near, (mine_ref, theirs_ref, out_ref, sems) = refs[:NX], refs[NX:]
    core, reads = at_ref[1], out_ref.shape[1]
    for distance in range(NX):
        column = at_distance(at_ref, distance)
        for read in range(reads):
            block = near[distance][read // NEIGH, read % NEIGH]
            row, same = lax.rem(block // NC, NY), lax.rem(block, NC) == core
            sem = sems.at[distance * reads + read]

            @pl.when(same)
            def _():
                pltpu.make_async_copy(mine_ref.at[row], out_ref.at[column, read], sem).start()

            @pl.when(jnp.logical_not(same))
            def _():
                pltpu.make_async_copy(theirs_ref.at[row], out_ref.at[column, read], sem).start()

    for count in range(NX * reads):
        place = out_ref.at[count // reads, count % reads]
        pltpu.make_async_copy(mine_ref.at[0], place, sems.at[count]).wait()


def spread_kernel(ids_ref, from_ref, out_ref):
    reads = from_ref.shape[1]
    spans = reads // NEIGH
    for read in range(reads):
        owner = ids_ref[read // NEIGH, read % NEIGH]
        block = from_ref[owner // (NY * NC), read]
        for at in range(read // NEIGH, NZ, spans):
            out_ref[at, read % NEIGH] = block


def owner_kernel(at_ref, *refs):
    near, (from_ref, mine_ref, theirs_ref, total) = refs[:NX], refs[NX:]
    total[...] = jnp.zeros_like(total)
    here, core = at_ref[0], at_ref[1]
    for distance in range(NX):
        column = at_distance(at_ref, distance)
        for read in range(from_ref.shape[1]):
            block = near[distance][read // NEIGH, read % NEIGH]

            @pl.when(block // (NY * NC) == here)
            def _():
                side = jnp.where(lax.rem(block, NC) == core, 0, NY)
                at = side + lax.rem(block // NC, NY)
                total[at] = total[at] + from_ref[column, read].astype(F32)

    mine_ref[...] = total[:NY]
    theirs_ref[...] = total[NY:].astype(BF16)


def attention_kernel(
    tok, w_own, q_own, g_own, from_pair, kc, ks, qc, qs, w_far,
    part, dq_own, dq_pair, dk_all, dv_all, w_pair, sem,
):
    fetch = pltpu.make_async_copy(w_far, w_pair, sem)
    fetch.start()
    scale = 1.0 / math.sqrt(HEAD)
    half = HEAD // 2
    width = w_own.shape[2]
    rows = jnp.concatenate([tok[:, n].reshape(NLEN, DE) for n in range(NEIGH)], axis=0)
    projected = [(dot(rows, w_own[0]), dot(rows, w_own[1]).astype(BF16))]
    fetch.wait()
    projected.append((dot(rows, w_pair[0]), dot(rows, w_pair[1]).astype(BF16)))
    key_cos, key_sin, query_cos, query_sin = kc[...], ks[...], qc[...], qs[...]
    for turn, (q, g, dq) in enumerate((
        (q_own, g_own, dq_own),
        (from_pair.at[:SPAN], from_pair.at[SPAN:], dq_pair),
    )):
        key_raw, values = projected[turn]
        for head in range(width // HEAD):
            cols = slice(head * HEAD, (head + 1) * HEAD)
            place = slice(turn * width + head * HEAD, turn * width + (head + 1) * HEAD)
            raw = key_raw[:, cols]
            key = (raw * key_cos + pltpu.roll(raw, half, 1) * key_sin).astype(BF16)
            value = values[:, cols]
            wide = q[:, cols].astype(F32)
            query = (wide * query_cos + pltpu.roll(wide, half, 1) * query_sin).astype(BF16)
            grad = g[:, cols]
            exponentials = jnp.exp(dot(query, key, (1, 1)) * scale)
            weights = exponentials / jnp.sum(exponentials, axis=-1, keepdims=True)
            weights_low = weights.astype(BF16)
            grad_weights = dot(grad, value, (1, 1))
            delta = jnp.sum(weights_low.astype(F32) * grad_weights, axis=-1, keepdims=True)
            grad_scores = (weights * (grad_weights - delta) * scale).astype(BF16)
            dv_all[:, place] = dot(weights_low, grad, (0, 0)).astype(BF16)
            grad_query = dot(grad_scores, key)
            dq[:, cols] = (
                grad_query * query_cos - pltpu.roll(grad_query, half, 1) * query_sin
            ).astype(BF16)
            grad_key = dot(grad_scores, query, (0, 0))
            dk_all[:, place] = (
                grad_key * key_cos - pltpu.roll(grad_key, half, 1) * key_sin
            ).astype(BF16)
    product = dot(dk_all[:, :width], w_own[0], (1, 1)) + dot(dv_all[:, :width], w_own[1], (1, 1))
    product = product + dot(dk_all[:, width:], w_pair[0], (1, 1))
    product = product + dot(dv_all[:, width:], w_pair[1], (1, 1))
    for n in range(NEIGH):
        piece = product[n * NLEN:(n + 1) * NLEN].astype(BF16)
        part[:, n] = piece.reshape(NZ, ROWS, DE)


def on_core(kernel, name, shapes, scalars, *operands, scratch=(), space=VMEM):
    return pl.pallas_call(
        kernel,
        out_shape=shapes,
        in_specs=[SMEM] * len(scalars) + [space] * len(operands),
        out_specs=jax.tree.map(lambda _: space, shapes),
        scratch_shapes=scratch,
        compiler_params=pltpu.CompilerParams(vmem_limit_bytes=16 << 20),
        name=name,
    )(*scalars, *operands)


def attention(*operands):
    _, depth, width = operands[1].shape
    return pl.pallas_call(
        attention_kernel,
        out_shape=(
            jax.ShapeDtypeStruct((NZ, NEIGH, ROWS, DE), BF16),
            jax.ShapeDtypeStruct((SPAN, width), BF16),
            jax.ShapeDtypeStruct((SPAN, width), BF16),
        ),
        in_specs=[VMEM] * (len(operands) - 1) + [ANY],
        out_specs=(VMEM, VMEM, VMEM),
        scratch_shapes=[
            pltpu.VMEM((NEIGH * NLEN, 2 * width), BF16),
            pltpu.VMEM((NEIGH * NLEN, 2 * width), BF16),
            pltpu.VMEM((2, depth, width), BF16),
            pltpu.SemaphoreType.DMA,
        ],
        compiler_params=pltpu.CompilerParams(vmem_limit_bytes=40 << 20),
        cost_estimate=pl.CostEstimate(
            flops=2_100_000_000, bytes_accessed=6_000_000, transcendentals=131072
        ),
        name="attention",
    )(*operands)


def local(queries, out_grad, encodings, kv_weight, neighbour_ids, rot_offset):
    x_at, c_at, z_at = lax.axis_index("x"), lax.axis_index("c"), lax.axis_index("z")
    spans = neighbour_ids.shape[0]
    reads = spans * NEIGH
    span_at = z_at % 2

    w_far = swapped(kv_weight, "z", NZ)
    rows_q = queries.reshape(spans, SPAN, -1)
    rows_g = out_grad.reshape(spans, SPAN, -1)
    other = jnp.concatenate(
        [
            lax.dynamic_index_in_dim(rows_q, 1 - span_at, 0, keepdims=False),
            lax.dynamic_index_in_dim(rows_g, 1 - span_at, 0, keepdims=False),
        ],
        axis=0,
    )
    q_own = lax.dynamic_index_in_dim(rows_q, span_at, 0, keepdims=False)
    g_own = lax.dynamic_index_in_dim(rows_g, span_at, 0, keepdims=False)
    offsets = lax.dynamic_index_in_dim(rot_offset, span_at, 0, keepdims=False)
    positions = offsets[:, None] + jnp.arange(NLEN, dtype=jnp.int32)[None, :]
    key_cos, key_sin = rotary_tables(positions.reshape(NEIGH * NLEN))
    query_cos, query_sin = rotary_tables(jnp.arange(SPAN, dtype=jnp.int32))

    at = jnp.stack([x_at, c_at])
    near = [neighbour_ids] + [shifted(neighbour_ids, "x", NX, s) for s in range(1, NX)]
    copies = jnp.broadcast_to(encodings, (NY, ROWS, DE))
    over_y = lax.all_to_all(copies, "y", split_axis=0, concat_axis=0, tiled=True)
    over_y, near, other = lax.optimization_barrier((over_y, near, other))
    beside = swapped(over_y, "c", NC)
    block = (reads, ROWS, DE)
    asked = on_core(
        pick_kernel, "pick", jax.ShapeDtypeStruct((NX, *block), BF16), (at, *near),
        over_y, beside, scratch=[pltpu.SemaphoreType.DMA((NX * reads,))], space=ANY,
    )
    found = lax.all_to_all(asked, "x", split_axis=0, concat_axis=0, tiled=True)

    to_z = on_core(
        spread_kernel, "spread", jax.ShapeDtypeStruct((NZ, NEIGH, ROWS, DE), BF16), (neighbour_ids,),
        found,
    )
    from_pair = swapped(other, "z", NZ)
    to_z, w_far, from_pair = lax.optimization_barrier((to_z, w_far, from_pair))
    tok = lax.all_to_all(to_z, "z", split_axis=0, concat_axis=0, tiled=True)
    part, dq_own, dq_pair = attention(
        tok, kv_weight, q_own, g_own, from_pair,
        key_cos, key_sin, query_cos, query_sin, w_far,
    )

    from_heads = lax.all_to_all(part, "z", split_axis=0, concat_axis=0, tiled=True)
    from_heads = from_heads.reshape(NZ // spans, spans, NEIGH, ROWS, DE)
    read_sum = jnp.sum(from_heads.astype(F32), axis=0).astype(BF16).reshape(reads, ROWS, DE)

    read_copies = jnp.broadcast_to(read_sum, (NX, *block))
    read_copies, dq_pair = lax.optimization_barrier((read_copies, dq_pair))
    read_x = lax.all_to_all(read_copies, "x", split_axis=0, concat_axis=0, tiled=True)
    dq_back = swapped(dq_pair, "z", NZ)
    first = jnp.where(span_at == 0, dq_own, dq_back)
    second = jnp.where(span_at == 0, dq_back, dq_own)
    grad_query = jnp.concatenate([first, second], axis=0)
    read_x, grad_query = lax.optimization_barrier((read_x, grad_query))
    owners = (NY, ROWS, DE)
    mine, theirs = on_core(
        owner_kernel, "owner_sums",
        (jax.ShapeDtypeStruct(owners, F32), jax.ShapeDtypeStruct(owners, BF16)),
        (at, *near), read_x, scratch=[pltpu.VMEM((NC * NY, ROWS, DE), F32)],
    )
    owner_part = (mine + swapped(theirs, "c", NC).astype(F32)).astype(BF16)
    from_y = lax.all_to_all(owner_part, "y", split_axis=0, concat_axis=0, tiled=True)
    owned = jnp.sum(from_y.astype(F32), axis=0)
    return (grad_query, owned.reshape(1, ROWS, DE))


def solution(mesh):
    fine = Mesh(mesh.devices.reshape(NX, NY, NC, NZ), ("x", "y", "c", "z"))
    enc = ("x", "y", "c")
    in_specs = (
        P(enc, "z"),
        P(enc, "z"),
        P(enc, "z", None),
        P(None, None, "z"),
        P(enc, None),
        P(enc, None),
    )
    out_specs = (P(enc, "z"), P(enc, "z", None))
    return jax.shard_map(local, mesh=fine, in_specs=in_specs, out_specs=out_specs, check_vma=False)
```

```python
import math

import jax
import jax.numpy as jnp
from jax import lax
from jax.experimental import pallas as pl
from jax.experimental.pallas import tpu as pltpu
from jax.sharding import Mesh, PartitionSpec as P

HEAD = 128
DE = 896
SPAN = 64
NEIGH = 2
NLEN = 128
NX, NY, NC, NZ = 4, 8, 2, 8
ROWS = NLEN // NZ
F32, BF16 = jnp.float32, jnp.bfloat16
VMEM = pl.BlockSpec(memory_space=pltpu.VMEM)
SMEM = pl.BlockSpec(memory_space=pltpu.SMEM)
ANY = pl.BlockSpec(memory_space=pl.ANY)


def rotary_tables(positions):
    halfway = HEAD // 2
    exponent = jnp.arange(halfway, dtype=F32) * (2.0 / HEAD)
    frequency = jnp.exp(-math.log(10000.0) * exponent)
    angles = positions.astype(F32)[:, None] * frequency[None, :]
    cosine, sine = jnp.cos(angles), jnp.sin(angles)
    return jnp.concatenate([cosine, cosine], axis=-1), jnp.concatenate([-sine, sine], axis=-1)


def shifted(value, axis, size, shift):
    return lax.ppermute(value, axis, [(i, (i + shift) % size) for i in range(size)])


def swapped(value, axis, size):
    return lax.ppermute(value, axis, [(i, i ^ 1) for i in range(size)])


def dot(a, b, over=(1, 0)):
    return lax.dot_general(
        a, b, (((over[0],), (over[1],)), ((), ())), preferred_element_type=F32
    )


def at_distance(at_ref, distance):
    return lax.rem(at_ref[0] - distance + NX, NX)


def pick_kernel(at_ref, *refs):
    near, (mine_ref, theirs_ref, out_ref, sems) = refs[:NX], refs[NX:]
    core, reads = at_ref[1], out_ref.shape[1]
    for distance in range(NX):
        column = at_distance(at_ref, distance)
        for read in range(reads):
            block = near[distance][read // NEIGH, read % NEIGH]
            row, same = lax.rem(block // NC, NY), lax.rem(block, NC) == core
            sem = sems.at[distance * reads + read]

            @pl.when(same)
            def _():
                pltpu.make_async_copy(mine_ref.at[row], out_ref.at[column, read], sem).start()

            @pl.when(jnp.logical_not(same))
            def _():
                pltpu.make_async_copy(theirs_ref.at[row], out_ref.at[column, read], sem).start()

    for count in range(NX * reads):
        place = out_ref.at[count // reads, count % reads]
        pltpu.make_async_copy(mine_ref.at[0], place, sems.at[count]).wait()


def spread_kernel(ids_ref, from_ref, out_ref):
    reads = from_ref.shape[1]
    spans = reads // NEIGH
    for read in range(reads):
        owner = ids_ref[read // NEIGH, read % NEIGH]
        block = from_ref[owner // (NY * NC), read]
        for at in range(read // NEIGH, NZ, spans):
            out_ref[at, read % NEIGH] = block


def owner_kernel(at_ref, *refs):
    near, (from_ref, mine_ref, theirs_ref, total) = refs[:NX], refs[NX:]
    total[...] = jnp.zeros_like(total)
    here, core = at_ref[0], at_ref[1]
    for distance in range(NX):
        column = at_distance(at_ref, distance)
        for read in range(from_ref.shape[1]):
            block = near[distance][read // NEIGH, read % NEIGH]

            @pl.when(block // (NY * NC) == here)
            def _():
                side = jnp.where(lax.rem(block, NC) == core, 0, NY)
                at = side + lax.rem(block // NC, NY)
                total[at] = total[at] + from_ref[column, read].astype(F32)

    mine_ref[...] = total[:NY]
    theirs_ref[...] = total[NY:].astype(BF16)


def attention_kernel(
    tok, w_own, q_own, g_own, from_pair, kc, ks, qc, qs, w_far,
    part, dq_own, dq_pair, dk_all, dv_all, w_pair, sem,
):
    fetch = pltpu.make_async_copy(w_far, w_pair, sem)
    fetch.start()
    scale = 1.0 / math.sqrt(HEAD)
    half = HEAD // 2
    width = w_own.shape[2]
    rows = jnp.concatenate([tok[:, n].reshape(NLEN, DE) for n in range(NEIGH)], axis=0)
    projected = [(dot(rows, w_own[0]), dot(rows, w_own[1]).astype(BF16))]
    fetch.wait()
    projected.append((dot(rows, w_pair[0]), dot(rows, w_pair[1]).astype(BF16)))
    key_cos, key_sin, query_cos, query_sin = kc[...], ks[...], qc[...], qs[...]
    for turn, (q, g, dq) in enumerate((
        (q_own, g_own, dq_own),
        (from_pair.at[:SPAN], from_pair.at[SPAN:], dq_pair),
    )):
        key_raw, values = projected[turn]
        for head in range(width // HEAD):
            cols = slice(head * HEAD, (head + 1) * HEAD)
            place = slice(turn * width + head * HEAD, turn * width + (head + 1) * HEAD)
            raw = key_raw[:, cols]
            key = (raw * key_cos + pltpu.roll(raw, half, 1) * key_sin).astype(BF16)
            value = values[:, cols]
            wide = q[:, cols].astype(F32)
            query = (wide * query_cos + pltpu.roll(wide, half, 1) * query_sin).astype(BF16)
            grad = g[:, cols]
            exponentials = jnp.exp(dot(query, key, (1, 1)) * scale)
            weights = exponentials / jnp.sum(exponentials, axis=-1, keepdims=True)
            weights_low = weights.astype(BF16)
            grad_weights = dot(grad, value, (1, 1))
            delta = jnp.sum(weights_low.astype(F32) * grad_weights, axis=-1, keepdims=True)
            grad_scores = (weights * (grad_weights - delta) * scale).astype(BF16)
            dv_all[:, place] = dot(weights_low, grad, (0, 0)).astype(BF16)
            grad_query = dot(grad_scores, key)
            dq[:, cols] = (
                grad_query * query_cos - pltpu.roll(grad_query, half, 1) * query_sin
            ).astype(BF16)
            grad_key = dot(grad_scores, query, (0, 0))
            dk_all[:, place] = (
                grad_key * key_cos - pltpu.roll(grad_key, half, 1) * key_sin
            ).astype(BF16)
    product = dot(dk_all[:, :width], w_own[0], (1, 1)) + dot(dv_all[:, :width], w_own[1], (1, 1))
    product = product + dot(dk_all[:, width:], w_pair[0], (1, 1))
    product = product + dot(dv_all[:, width:], w_pair[1], (1, 1))
    for n in range(NEIGH):
        piece = product[n * NLEN:(n + 1) * NLEN].astype(BF16)
        part[:, n] = piece.reshape(NZ, ROWS, DE)


def on_core(kernel, name, shapes, scalars, *operands, scratch=(), space=VMEM):
    return pl.pallas_call(
        kernel,
        out_shape=shapes,
        in_specs=[SMEM] * len(scalars) + [space] * len(operands),
        out_specs=jax.tree.map(lambda _: space, shapes),
        scratch_shapes=scratch,
        compiler_params=pltpu.CompilerParams(vmem_limit_bytes=16 << 20),
        name=name,
    )(*scalars, *operands)


def attention(*operands):
    _, depth, width = operands[1].shape
    return pl.pallas_call(
        attention_kernel,
        out_shape=(
            jax.ShapeDtypeStruct((NZ, NEIGH, ROWS, DE), BF16),
            jax.ShapeDtypeStruct((SPAN, width), BF16),
            jax.ShapeDtypeStruct((SPAN, width), BF16),
        ),
        in_specs=[VMEM] * (len(operands) - 1) + [ANY],
        out_specs=(VMEM, VMEM, VMEM),
        scratch_shapes=[
            pltpu.VMEM((NEIGH * NLEN, 2 * width), BF16),
            pltpu.VMEM((NEIGH * NLEN, 2 * width), BF16),
            pltpu.VMEM((2, depth, width), BF16),
            pltpu.SemaphoreType.DMA,
        ],
        compiler_params=pltpu.CompilerParams(vmem_limit_bytes=40 << 20),
        cost_estimate=pl.CostEstimate(
            flops=2_100_000_000, bytes_accessed=6_000_000, transcendentals=131072
        ),
        name="attention",
    )(*operands)


def local(queries, out_grad, encodings, kv_weight, neighbour_ids, rot_offset):
    x_at, c_at, z_at = lax.axis_index("x"), lax.axis_index("c"), lax.axis_index("z")
    spans = neighbour_ids.shape[0]
    reads = spans * NEIGH
    span_at = z_at % 2

    w_far = swapped(kv_weight, "z", NZ)
    rows_q = queries.reshape(spans, SPAN, -1)
    rows_g = out_grad.reshape(spans, SPAN, -1)
    other = jnp.concatenate(
        [
            lax.dynamic_index_in_dim(rows_q, 1 - span_at, 0, keepdims=False),
            lax.dynamic_index_in_dim(rows_g, 1 - span_at, 0, keepdims=False),
        ],
        axis=0,
    )
    q_own = lax.dynamic_index_in_dim(rows_q, span_at, 0, keepdims=False)
    g_own = lax.dynamic_index_in_dim(rows_g, span_at, 0, keepdims=False)
    offsets = lax.dynamic_index_in_dim(rot_offset, span_at, 0, keepdims=False)
    positions = offsets[:, None] + jnp.arange(NLEN, dtype=jnp.int32)[None, :]
    key_cos, key_sin = rotary_tables(positions.reshape(NEIGH * NLEN))
    query_cos, query_sin = rotary_tables(jnp.arange(SPAN, dtype=jnp.int32))

    at = jnp.stack([x_at, c_at])
    near = [neighbour_ids] + [shifted(neighbour_ids, "x", NX, s) for s in range(1, NX)]
    copies = jnp.broadcast_to(encodings, (NY, ROWS, DE))
    over_y = lax.all_to_all(copies, "y", split_axis=0, concat_axis=0, tiled=True)
    over_y, near[:-1], other = lax.optimization_barrier((over_y, near[:-1], other))
    beside = swapped(over_y, "c", NC)
    block = (reads, ROWS, DE)
    asked = on_core(
        pick_kernel, "pick", jax.ShapeDtypeStruct((NX, *block), BF16), (at, *near),
        over_y, beside, scratch=[pltpu.SemaphoreType.DMA((NX * reads,))], space=ANY,
    )
    found = lax.all_to_all(asked, "x", split_axis=0, concat_axis=0, tiled=True)

    to_z = on_core(
        spread_kernel, "spread", jax.ShapeDtypeStruct((NZ, NEIGH, ROWS, DE), BF16), (neighbour_ids,),
        found,
    )
    from_pair = swapped(other, "z", NZ)
    to_z, w_far, from_pair = lax.optimization_barrier((to_z, w_far, from_pair))
    tok = lax.all_to_all(to_z, "z", split_axis=0, concat_axis=0, tiled=True)
    part, dq_own, dq_pair = attention(
        tok, kv_weight, q_own, g_own, from_pair,
        key_cos, key_sin, query_cos, query_sin, w_far,
    )

    from_heads = lax.all_to_all(part, "z", split_axis=0, concat_axis=0, tiled=True)
    from_heads = from_heads.reshape(NZ // spans, spans, NEIGH, ROWS, DE)
    read_sum = jnp.sum(from_heads.astype(F32), axis=0).astype(BF16).reshape(reads, ROWS, DE)

    read_copies = jnp.broadcast_to(read_sum, (NX, *block))
    read_copies, dq_pair = lax.optimization_barrier((read_copies, dq_pair))
    read_x = lax.all_to_all(read_copies, "x", split_axis=0, concat_axis=0, tiled=True)
    dq_back = swapped(dq_pair, "z", NZ)
    read_x, dq_back = lax.optimization_barrier((read_x, dq_back))
    first = jnp.where(span_at == 0, dq_own, dq_back)
    second = jnp.where(span_at == 0, dq_back, dq_own)
    grad_query = jnp.concatenate([first, second], axis=0)
    owners = (NY, ROWS, DE)
    mine, theirs = on_core(
        owner_kernel, "owner_sums",
        (jax.ShapeDtypeStruct(owners, F32), jax.ShapeDtypeStruct(owners, BF16)),
        (at, *near), read_x, scratch=[pltpu.VMEM((NC * NY, ROWS, DE), F32)],
    )
    owner_part = (mine + swapped(theirs, "c", NC).astype(F32)).astype(BF16)
    owner_part, grad_query = lax.optimization_barrier((owner_part, grad_query))
    from_y = lax.all_to_all(owner_part, "y", split_axis=0, concat_axis=0, tiled=True)
    owned = jnp.sum(from_y.astype(F32), axis=0)
    return (grad_query, owned.reshape(1, ROWS, DE))


def solution(mesh):
    fine = Mesh(mesh.devices.reshape(NX, NY, NC, NZ), ("x", "y", "c", "z"))
    enc = ("x", "y", "c")
    in_specs = (
        P(enc, "z"),
        P(enc, "z"),
        P(enc, "z", None),
        P(None, None, "z"),
        P(enc, None),
        P(enc, None),
    )
    out_specs = (P(enc, "z"), P(enc, "z", None))
    return jax.shard_map(local, mesh=fine, in_specs=in_specs, out_specs=out_specs, check_vma=False)
```

```python
import math

import jax
import jax.numpy as jnp
from jax import lax
from jax.experimental import pallas as pl
from jax.experimental.pallas import tpu as pltpu
from jax.sharding import Mesh, PartitionSpec as P

HEAD = 128
DE = 896
SPAN = 64
NEIGH = 2
NLEN = 128
NX, NY, NC, NZ = 4, 8, 2, 8
FETCHES = 4
ROWS = NLEN // NZ
F32, BF16 = jnp.float32, jnp.bfloat16
VMEM = pl.BlockSpec(memory_space=pltpu.VMEM)
SMEM = pl.BlockSpec(memory_space=pltpu.SMEM)
ANY = pl.BlockSpec(memory_space=pl.ANY)


def rotary_tables(positions):
    halfway = HEAD // 2
    exponent = jnp.arange(halfway, dtype=F32) * (2.0 / HEAD)
    frequency = jnp.exp(-math.log(10000.0) * exponent)
    angles = positions.astype(F32)[:, None] * frequency[None, :]
    cosine, sine = jnp.cos(angles), jnp.sin(angles)
    return jnp.concatenate([cosine, cosine], axis=-1), jnp.concatenate([-sine, sine], axis=-1)


def shifted(value, axis, size, shift):
    return lax.ppermute(value, axis, [(i, (i + shift) % size) for i in range(size)])


def swapped(value, axis, size):
    return lax.ppermute(value, axis, [(i, i ^ 1) for i in range(size)])


def dot(a, b, over=(1, 0)):
    return lax.dot_general(
        a, b, (((over[0],), (over[1],)), ((), ())), preferred_element_type=F32
    )


def read_id(at_ref, near, distance, read):
    if distance == 0:
        return at_ref[2 + read]
    return near[distance - 1][read // NEIGH, read % NEIGH]


def at_distance(at_ref, distance):
    return lax.rem(at_ref[0] - distance + NX, NX)


def pick_kernel(at_ref, *refs):
    near, (mine_ref, theirs_ref, out_ref, sems) = refs[:NX - 1], refs[NX - 1:]
    core, reads = at_ref[1], out_ref.shape[1]
    for distance in range(NX):
        column = at_distance(at_ref, distance)
        for read in range(reads):
            block = read_id(at_ref, near, distance, read)
            row, same = lax.rem(block // NC, NY), lax.rem(block, NC) == core
            sem = sems.at[distance * reads + read]

            @pl.when(same)
            def _():
                pltpu.make_async_copy(mine_ref.at[row], out_ref.at[column, read], sem).start()

            @pl.when(jnp.logical_not(same))
            def _():
                pltpu.make_async_copy(theirs_ref.at[row], out_ref.at[column, read], sem).start()

    for count in range(NX * reads):
        place = out_ref.at[count // reads, count % reads]
        pltpu.make_async_copy(mine_ref.at[0], place, sems.at[count]).wait()


def spread_kernel(at_ref, from_ref, out_ref):
    reads = from_ref.shape[1]
    spans = reads // NEIGH
    for read in range(reads):
        owner = at_ref[2 + read]
        block = from_ref[owner // (NY * NC), read]
        for at in range(read // NEIGH, NZ, spans):
            out_ref[at, read % NEIGH] = block


def owner_kernel(at_ref, *refs):
    near, (from_ref, mine_ref, theirs_ref, total) = refs[:NX - 1], refs[NX - 1:]
    total[...] = jnp.zeros_like(total)
    here, core = at_ref[0], at_ref[1]
    for distance in range(NX):
        column = at_distance(at_ref, distance)
        for read in range(from_ref.shape[1]):
            block = read_id(at_ref, near, distance, read)

            @pl.when(block // (NY * NC) == here)
            def _():
                side = jnp.where(lax.rem(block, NC) == core, 0, NY)
                at = side + lax.rem(block // NC, NY)
                total[at] = total[at] + from_ref[column, read].astype(F32)

    mine_ref[...] = total[:NY]
    theirs_ref[...] = total[NY:].astype(BF16)


def attention_kernel(
    tok, w_own, q_own, g_own, from_pair, kc, ks, qc, qs, w_far,
    part, dq_own, dq_pair, dk_all, dv_all, w_pair, sems,
):
    step = w_own.shape[1] // FETCHES
    fetches = [
        [
            pltpu.make_async_copy(
                w_far.at[part_at, pl.ds(i * step, step)],
                w_pair.at[part_at, pl.ds(i * step, step)],
                sems.at[part_at, i],
            )
            for i in range(FETCHES)
        ]
        for part_at in range(2)
    ]
    for fetch in fetches[0] + fetches[1]:
        fetch.start()
    scale = 1.0 / math.sqrt(HEAD)
    half = HEAD // 2
    width = w_own.shape[2]
    rows = jnp.concatenate([tok[:, n].reshape(NLEN, DE) for n in range(NEIGH)], axis=0)
    key_cos, key_sin, query_cos, query_sin = kc[...], ks[...], qc[...], qs[...]

    def heads(turn, key_raw, values, q, g, dq):
        for head in range(width // HEAD):
            cols = slice(head * HEAD, (head + 1) * HEAD)
            place = slice(turn * width + head * HEAD, turn * width + (head + 1) * HEAD)
            raw = key_raw[:, cols]
            key = (raw * key_cos + pltpu.roll(raw, half, 1) * key_sin).astype(BF16)
            value = values[:, cols]
            wide = q[:, cols].astype(F32)
            query = (wide * query_cos + pltpu.roll(wide, half, 1) * query_sin).astype(BF16)
            grad = g[:, cols]
            exponentials = jnp.exp(dot(query, key, (1, 1)) * scale)
            weights = exponentials / jnp.sum(exponentials, axis=-1, keepdims=True)
            weights_low = weights.astype(BF16)
            grad_weights = dot(grad, value, (1, 1))
            delta = jnp.sum(weights_low.astype(F32) * grad_weights, axis=-1, keepdims=True)
            grad_scores = (weights * (grad_weights - delta) * scale).astype(BF16)
            dv_all[:, place] = dot(weights_low, grad, (0, 0)).astype(BF16)
            grad_query = dot(grad_scores, key)
            dq[:, cols] = (
                grad_query * query_cos - pltpu.roll(grad_query, half, 1) * query_sin
            ).astype(BF16)
            grad_key = dot(grad_scores, query, (0, 0))
            dk_all[:, place] = (
                grad_key * key_cos - pltpu.roll(grad_key, half, 1) * key_sin
            ).astype(BF16)

    key_own, values_own = dot(rows, w_own[0]), dot(rows, w_own[1]).astype(BF16)
    for fetch in fetches[0]:
        fetch.wait()
    key_pair = dot(rows, w_pair[0])
    heads(0, key_own, values_own, q_own, g_own, dq_own)
    for fetch in fetches[1]:
        fetch.wait()
    values_pair = dot(rows, w_pair[1]).astype(BF16)
    heads(1, key_pair, values_pair, from_pair.at[:SPAN], from_pair.at[SPAN:], dq_pair)
    product = dot(dk_all[:, :width], w_own[0], (1, 1)) + dot(dv_all[:, :width], w_own[1], (1, 1))
    product = product + dot(dk_all[:, width:], w_pair[0], (1, 1))
    product = product + dot(dv_all[:, width:], w_pair[1], (1, 1))
    for n in range(NEIGH):
        piece = product[n * NLEN:(n + 1) * NLEN].astype(BF16)
        part[:, n] = piece.reshape(NZ, ROWS, DE)


def on_core(kernel, name, shapes, scalars, *operands, scratch=(), space=VMEM):
    return pl.pallas_call(
        kernel,
        out_shape=shapes,
        in_specs=[SMEM] * len(scalars) + [space] * len(operands),
        out_specs=jax.tree.map(lambda _: space, shapes),
        scratch_shapes=scratch,
        compiler_params=pltpu.CompilerParams(vmem_limit_bytes=16 << 20),
        name=name,
    )(*scalars, *operands)


def attention(*operands):
    _, depth, width = operands[1].shape
    return pl.pallas_call(
        attention_kernel,
        out_shape=(
            jax.ShapeDtypeStruct((NZ, NEIGH, ROWS, DE), BF16),
            jax.ShapeDtypeStruct((SPAN, width), BF16),
            jax.ShapeDtypeStruct((SPAN, width), BF16),
        ),
        in_specs=[VMEM] * (len(operands) - 1) + [ANY],
        out_specs=(VMEM, VMEM, VMEM),
        scratch_shapes=[
            pltpu.VMEM((NEIGH * NLEN, 2 * width), BF16),
            pltpu.VMEM((NEIGH * NLEN, 2 * width), BF16),
            pltpu.VMEM((2, depth, width), BF16),
            pltpu.SemaphoreType.DMA((2, FETCHES)),
        ],
        compiler_params=pltpu.CompilerParams(vmem_limit_bytes=40 << 20),
        cost_estimate=pl.CostEstimate(
            flops=2_100_000_000, bytes_accessed=6_000_000, transcendentals=131072
        ),
        name="attention",
    )(*operands)


def local(queries, out_grad, encodings, kv_weight, neighbour_ids, rot_offset):
    x_at, c_at, z_at = lax.axis_index("x"), lax.axis_index("c"), lax.axis_index("z")
    spans = neighbour_ids.shape[0]
    reads = spans * NEIGH
    span_at = z_at % 2

    w_far = swapped(kv_weight, "z", NZ)
    rows_q = queries.reshape(spans, SPAN, -1)
    rows_g = out_grad.reshape(spans, SPAN, -1)
    other = jnp.concatenate(
        [
            lax.dynamic_index_in_dim(rows_q, 1 - span_at, 0, keepdims=False),
            lax.dynamic_index_in_dim(rows_g, 1 - span_at, 0, keepdims=False),
        ],
        axis=0,
    )
    q_own = lax.dynamic_index_in_dim(rows_q, span_at, 0, keepdims=False)
    g_own = lax.dynamic_index_in_dim(rows_g, span_at, 0, keepdims=False)
    offsets = lax.dynamic_index_in_dim(rot_offset, span_at, 0, keepdims=False)
    positions = offsets[:, None] + jnp.arange(NLEN, dtype=jnp.int32)[None, :]
    key_cos, key_sin = rotary_tables(positions.reshape(NEIGH * NLEN))
    query_cos, query_sin = rotary_tables(jnp.arange(SPAN, dtype=jnp.int32))

    at = jnp.concatenate([x_at.reshape(1), c_at.reshape(1), neighbour_ids.reshape(reads)])
    near = [shifted(neighbour_ids, "x", NX, s) for s in range(1, NX)]
    copies = jnp.broadcast_to(encodings, (NY, ROWS, DE))
    over_y = lax.all_to_all(copies, "y", split_axis=0, concat_axis=0, tiled=True)
    over_y, near[:-1], other = lax.optimization_barrier((over_y, near[:-1], other))
    beside = swapped(over_y, "c", NC)
    block = (reads, ROWS, DE)
    asked = on_core(
        pick_kernel, "pick", jax.ShapeDtypeStruct((NX, *block), BF16), (at, *near),
        over_y, beside, scratch=[pltpu.SemaphoreType.DMA((NX * reads,))], space=ANY,
    )
    found = lax.all_to_all(asked, "x", split_axis=0, concat_axis=0, tiled=True)

    to_z = on_core(
        spread_kernel, "spread", jax.ShapeDtypeStruct((NZ, NEIGH, ROWS, DE), BF16), (at,),
        found,
    )
    from_pair = swapped(other, "z", NZ)
    to_z, w_far, from_pair = lax.optimization_barrier((to_z, w_far, from_pair))
    tok = lax.all_to_all(to_z, "z", split_axis=0, concat_axis=0, tiled=True)
    part, dq_own, dq_pair = attention(
        tok, kv_weight, q_own, g_own, from_pair,
        key_cos, key_sin, query_cos, query_sin, w_far,
    )

    from_heads = lax.all_to_all(part, "z", split_axis=0, concat_axis=0, tiled=True)
    from_heads = from_heads.reshape(NZ // spans, spans, NEIGH, ROWS, DE)
    read_sum = jnp.sum(from_heads.astype(F32), axis=0).astype(BF16).reshape(reads, ROWS, DE)

    read_copies = jnp.broadcast_to(read_sum, (NX, *block))
    read_copies, dq_pair = lax.optimization_barrier((read_copies, dq_pair))
    read_x = lax.all_to_all(read_copies, "x", split_axis=0, concat_axis=0, tiled=True)
    dq_back = swapped(dq_pair, "z", NZ)
    read_x, dq_back = lax.optimization_barrier((read_x, dq_back))
    first = jnp.where(span_at == 0, dq_own, dq_back)
    second = jnp.where(span_at == 0, dq_back, dq_own)
    grad_query = jnp.concatenate([first, second], axis=0)
    owners = (NY, ROWS, DE)
    mine, theirs = on_core(
        owner_kernel, "owner_sums",
        (jax.ShapeDtypeStruct(owners, F32), jax.ShapeDtypeStruct(owners, BF16)),
        (at, *near), read_x, scratch=[pltpu.VMEM((NC * NY, ROWS, DE), F32)],
    )
    owner_part = (mine + swapped(theirs, "c", NC).astype(F32)).astype(BF16)
    owner_part, grad_query = lax.optimization_barrier((owner_part, grad_query))
    from_y = lax.all_to_all(owner_part, "y", split_axis=0, concat_axis=0, tiled=True)
    owned = jnp.sum(from_y.astype(F32), axis=0)
    return (grad_query, owned.reshape(1, ROWS, DE))


def solution(mesh):
    fine = Mesh(mesh.devices.reshape(NX, NY, NC, NZ), ("x", "y", "c", "z"))
    enc = ("x", "y", "c")
    in_specs = (
        P(enc, "z"),
        P(enc, "z"),
        P(enc, "z", None),
        P(None, None, "z"),
        P(enc, None),
        P(enc, None),
    )
    out_specs = (P(enc, "z"), P(enc, "z", None))
    return jax.shard_map(local, mesh=fine, in_specs=in_specs, out_specs=out_specs, check_vma=False)
```

```python
import math

import jax
import jax.numpy as jnp
from jax import lax
from jax.experimental import pallas as pl
from jax.experimental.pallas import tpu as pltpu
from jax.sharding import Mesh, PartitionSpec as P

HEAD = 128
DE = 896
SPAN = 64
NEIGH = 2
NLEN = 128
NX, NY, NC, NZ = 4, 8, 2, 8
FETCHES = 4
ROWS = NLEN // NZ
F32, BF16 = jnp.float32, jnp.bfloat16
VMEM = pl.BlockSpec(memory_space=pltpu.VMEM)
SMEM = pl.BlockSpec(memory_space=pltpu.SMEM)
ANY = pl.BlockSpec(memory_space=pl.ANY)


def rotary_tables(positions):
    halfway = HEAD // 2
    exponent = jnp.arange(halfway, dtype=F32) * (2.0 / HEAD)
    frequency = jnp.exp(-math.log(10000.0) * exponent)
    angles = positions.astype(F32)[:, None] * frequency[None, :]
    cosine, sine = jnp.cos(angles), jnp.sin(angles)
    return jnp.concatenate([cosine, cosine], axis=-1), jnp.concatenate([-sine, sine], axis=-1)


def shifted(value, axis, size, shift):
    return lax.ppermute(value, axis, [(i, (i + shift) % size) for i in range(size)])


def swapped(value, axis, size):
    return lax.ppermute(value, axis, [(i, i ^ 1) for i in range(size)])


def dot(a, b, over=(1, 0)):
    return lax.dot_general(
        a, b, (((over[0],), (over[1],)), ((), ())), preferred_element_type=F32
    )


def read_id(at_ref, near, distance, read):
    if distance == 0:
        return at_ref[2 + read]
    return near[distance - 1][read // NEIGH, read % NEIGH]


def at_distance(at_ref, distance):
    return lax.rem(at_ref[0] - distance + NX, NX)


def pick_kernel(at_ref, *refs):
    near, (mine_ref, theirs_ref, out_ref, sems) = refs[:NX - 1], refs[NX - 1:]
    core, reads = at_ref[1], out_ref.shape[1]
    for distance in range(NX):
        column = at_distance(at_ref, distance)
        for read in range(reads):
            block = read_id(at_ref, near, distance, read)
            row, same = lax.rem(block // NC, NY), lax.rem(block, NC) == core
            sem = sems.at[distance * reads + read]

            @pl.when(same)
            def _():
                pltpu.make_async_copy(mine_ref.at[row], out_ref.at[column, read], sem).start()

            @pl.when(jnp.logical_not(same))
            def _():
                pltpu.make_async_copy(theirs_ref.at[row], out_ref.at[column, read], sem).start()

    for count in range(NX * reads):
        place = out_ref.at[count // reads, count % reads]
        pltpu.make_async_copy(mine_ref.at[0], place, sems.at[count]).wait()


def spread_kernel(at_ref, from_ref, out_ref):
    reads = from_ref.shape[1]
    spans = reads // NEIGH
    for read in range(reads):
        owner = at_ref[2 + read]
        block = from_ref[owner // (NY * NC), read]
        for at in range(read // NEIGH, NZ, spans):
            out_ref[at, read % NEIGH] = block


def owner_kernel(at_ref, *refs):
    near, (from_ref, mine_ref, theirs_ref, total) = refs[:NX - 1], refs[NX - 1:]
    total[...] = jnp.zeros_like(total)
    here, core = at_ref[0], at_ref[1]
    for distance in range(NX):
        column = at_distance(at_ref, distance)
        for read in range(from_ref.shape[1]):
            block = read_id(at_ref, near, distance, read)

            @pl.when(block // (NY * NC) == here)
            def _():
                side = jnp.where(lax.rem(block, NC) == core, 0, NY)
                at = side + lax.rem(block // NC, NY)
                total[at] = total[at] + from_ref[column, read].astype(F32)

    mine_ref[...] = total[:NY]
    theirs_ref[...] = total[NY:].astype(BF16)


def attention_kernel(
    tok, w_own, q_own, g_own, from_pair, kc, ks, qc, qs, w_far,
    part, dq_own, dq_pair, dk_all, dv_all, w_pair, sems,
):
    step = w_own.shape[1] // FETCHES
    fetches = [
        [
            pltpu.make_async_copy(
                w_far.at[part_at, pl.ds(i * step, step)],
                w_pair.at[part_at, pl.ds(i * step, step)],
                sems.at[part_at, i],
            )
            for i in range(FETCHES)
        ]
        for part_at in range(2)
    ]
    for fetch in fetches[0] + fetches[1]:
        fetch.start()
    scale = 1.0 / math.sqrt(HEAD)
    half = HEAD // 2
    width = w_own.shape[2]
    rows = jnp.concatenate([tok[:, n].reshape(NLEN, DE) for n in range(NEIGH)], axis=0)
    key_cos, key_sin, query_cos, query_sin = kc[...], ks[...], qc[...], qs[...]

    def heads(turn, key_raw, values, q, g, dq):
        for head in range(width // HEAD):
            cols = slice(head * HEAD, (head + 1) * HEAD)
            place = slice(turn * width + head * HEAD, turn * width + (head + 1) * HEAD)
            raw = key_raw[:, cols]
            key = (raw * key_cos + pltpu.roll(raw, half, 1) * key_sin).astype(BF16)
            value = values[:, cols]
            wide = q[:, cols].astype(F32)
            query = (wide * query_cos + pltpu.roll(wide, half, 1) * query_sin).astype(BF16)
            grad = g[:, cols]
            exponentials = jnp.exp(dot(query, key, (1, 1)) * scale)
            weights = exponentials / jnp.sum(exponentials, axis=-1, keepdims=True)
            weights_low = weights.astype(BF16)
            grad_weights = dot(grad, value, (1, 1))
            delta = jnp.sum(weights_low.astype(F32) * grad_weights, axis=-1, keepdims=True)
            grad_scores = (weights * (grad_weights - delta) * scale).astype(BF16)
            dv_all[:, place] = dot(weights_low, grad, (0, 0)).astype(BF16)
            grad_query = dot(grad_scores, key)
            dq[:, cols] = (
                grad_query * query_cos - pltpu.roll(grad_query, half, 1) * query_sin
            ).astype(BF16)
            grad_key = dot(grad_scores, query, (0, 0))
            dk_all[:, place] = (
                grad_key * key_cos - pltpu.roll(grad_key, half, 1) * key_sin
            ).astype(BF16)

    key_own, values_own = dot(rows, w_own[0]), dot(rows, w_own[1]).astype(BF16)
    for fetch in fetches[0] + fetches[1]:
        fetch.wait()
    key_pair, values_pair = dot(rows, w_pair[0]), dot(rows, w_pair[1]).astype(BF16)
    heads(0, key_own, values_own, q_own, g_own, dq_own)
    heads(1, key_pair, values_pair, from_pair.at[:SPAN], from_pair.at[SPAN:], dq_pair)
    product = dot(dk_all[:, :width], w_own[0], (1, 1)) + dot(dv_all[:, :width], w_own[1], (1, 1))
    product = product + dot(dk_all[:, width:], w_pair[0], (1, 1))
    product = product + dot(dv_all[:, width:], w_pair[1], (1, 1))
    for n in range(NEIGH):
        piece = product[n * NLEN:(n + 1) * NLEN].astype(BF16)
        part[:, n] = piece.reshape(NZ, ROWS, DE)


def on_core(kernel, name, shapes, scalars, *operands, scratch=(), space=VMEM):
    return pl.pallas_call(
        kernel,
        out_shape=shapes,
        in_specs=[SMEM] * len(scalars) + [space] * len(operands),
        out_specs=jax.tree.map(lambda _: space, shapes),
        scratch_shapes=scratch,
        compiler_params=pltpu.CompilerParams(vmem_limit_bytes=16 << 20),
        name=name,
    )(*scalars, *operands)


def attention(*operands):
    _, depth, width = operands[1].shape
    return pl.pallas_call(
        attention_kernel,
        out_shape=(
            jax.ShapeDtypeStruct((NZ, NEIGH, ROWS, DE), BF16),
            jax.ShapeDtypeStruct((SPAN, width), BF16),
            jax.ShapeDtypeStruct((SPAN, width), BF16),
        ),
        in_specs=[VMEM] * (len(operands) - 1) + [ANY],
        out_specs=(VMEM, VMEM, VMEM),
        scratch_shapes=[
            pltpu.VMEM((NEIGH * NLEN, 2 * width), BF16),
            pltpu.VMEM((NEIGH * NLEN, 2 * width), BF16),
            pltpu.VMEM((2, depth, width), BF16),
            pltpu.SemaphoreType.DMA((2, FETCHES)),
        ],
        compiler_params=pltpu.CompilerParams(vmem_limit_bytes=40 << 20),
        cost_estimate=pl.CostEstimate(
            flops=2_100_000_000, bytes_accessed=6_000_000, transcendentals=131072
        ),
        name="attention",
    )(*operands)


def local(queries, out_grad, encodings, kv_weight, neighbour_ids, rot_offset):
    x_at, c_at, z_at = lax.axis_index("x"), lax.axis_index("c"), lax.axis_index("z")
    spans = neighbour_ids.shape[0]
    reads = spans * NEIGH
    span_at = z_at % 2

    w_far = swapped(kv_weight, "z", NZ)
    rows_q = queries.reshape(spans, SPAN, -1)
    rows_g = out_grad.reshape(spans, SPAN, -1)
    other = jnp.concatenate(
        [
            lax.dynamic_index_in_dim(rows_q, 1 - span_at, 0, keepdims=False),
            lax.dynamic_index_in_dim(rows_g, 1 - span_at, 0, keepdims=False),
        ],
        axis=0,
    )
    q_own = lax.dynamic_index_in_dim(rows_q, span_at, 0, keepdims=False)
    g_own = lax.dynamic_index_in_dim(rows_g, span_at, 0, keepdims=False)
    offsets = lax.dynamic_index_in_dim(rot_offset, span_at, 0, keepdims=False)
    positions = offsets[:, None] + jnp.arange(NLEN, dtype=jnp.int32)[None, :]
    key_cos, key_sin = rotary_tables(positions.reshape(NEIGH * NLEN))
    query_cos, query_sin = rotary_tables(jnp.arange(SPAN, dtype=jnp.int32))

    at = jnp.concatenate([x_at.reshape(1), c_at.reshape(1), neighbour_ids.reshape(reads)])
    near = [shifted(neighbour_ids, "x", NX, s) for s in range(1, NX)]
    copies = jnp.broadcast_to(encodings, (NY, ROWS, DE))
    over_y = lax.all_to_all(copies, "y", split_axis=0, concat_axis=0, tiled=True)
    over_y, near[:-1], other, at = lax.optimization_barrier((over_y, near[:-1], other, at))
    beside = swapped(over_y, "c", NC)
    block = (reads, ROWS, DE)
    asked = on_core(
        pick_kernel, "pick", jax.ShapeDtypeStruct((NX, *block), BF16), (at, *near),
        over_y, beside, scratch=[pltpu.SemaphoreType.DMA((NX * reads,))], space=ANY,
    )
    found = lax.all_to_all(asked, "x", split_axis=0, concat_axis=0, tiled=True)

    to_z = on_core(
        spread_kernel, "spread", jax.ShapeDtypeStruct((NZ, NEIGH, ROWS, DE), BF16), (at,),
        found,
    )
    from_pair = swapped(other, "z", NZ)
    to_z, w_far, from_pair = lax.optimization_barrier((to_z, w_far, from_pair))
    tok = lax.all_to_all(to_z, "z", split_axis=0, concat_axis=0, tiled=True)
    part, dq_own, dq_pair = attention(
        tok, kv_weight, q_own, g_own, from_pair,
        key_cos, key_sin, query_cos, query_sin, w_far,
    )

    from_heads = lax.all_to_all(part, "z", split_axis=0, concat_axis=0, tiled=True)
    from_heads = from_heads.reshape(NZ // spans, spans, NEIGH, ROWS, DE)
    read_sum = jnp.sum(from_heads.astype(F32), axis=0).astype(BF16).reshape(reads, ROWS, DE)

    read_copies = jnp.broadcast_to(read_sum, (NX, *block))
    read_copies, dq_pair = lax.optimization_barrier((read_copies, dq_pair))
    read_x = lax.all_to_all(read_copies, "x", split_axis=0, concat_axis=0, tiled=True)
    dq_back = swapped(dq_pair, "z", NZ)
    read_x, dq_back = lax.optimization_barrier((read_x, dq_back))
    first = jnp.where(span_at == 0, dq_own, dq_back)
    second = jnp.where(span_at == 0, dq_back, dq_own)
    grad_query = jnp.concatenate([first, second], axis=0)
    owners = (NY, ROWS, DE)
    mine, theirs = on_core(
        owner_kernel, "owner_sums",
        (jax.ShapeDtypeStruct(owners, F32), jax.ShapeDtypeStruct(owners, BF16)),
        (at, *near), read_x, scratch=[pltpu.VMEM((NC * NY, ROWS, DE), F32)],
    )
    owner_part = (mine + swapped(theirs, "c", NC).astype(F32)).astype(BF16)
    owner_part, grad_query = lax.optimization_barrier((owner_part, grad_query))
    from_y = lax.all_to_all(owner_part, "y", split_axis=0, concat_axis=0, tiled=True)
    owned = jnp.sum(from_y.astype(F32), axis=0)
    return (grad_query, owned.reshape(1, ROWS, DE))


def solution(mesh):
    fine = Mesh(mesh.devices.reshape(NX, NY, NC, NZ), ("x", "y", "c", "z"))
    enc = ("x", "y", "c")
    in_specs = (
        P(enc, "z"),
        P(enc, "z"),
        P(enc, "z", None),
        P(None, None, "z"),
        P(enc, None),
        P(enc, None),
    )
    out_specs = (P(enc, "z"), P(enc, "z", None))
    return jax.shard_map(local, mesh=fine, in_specs=in_specs, out_specs=out_specs, check_vma=False)
```

```python
import math

import jax
import jax.numpy as jnp
from jax import lax
from jax.experimental import pallas as pl
from jax.experimental.pallas import tpu as pltpu
from jax.sharding import Mesh, PartitionSpec as P

HEAD = 128
DE = 896
SPAN = 64
NEIGH = 2
NLEN = 128
NX, NY, NC, NZ = 4, 8, 2, 8
ROWS = NLEN // NZ
F32, BF16 = jnp.float32, jnp.bfloat16
VMEM = pl.BlockSpec(memory_space=pltpu.VMEM)
SMEM = pl.BlockSpec(memory_space=pltpu.SMEM)
ANY = pl.BlockSpec(memory_space=pl.ANY)


def rotary_tables(positions):
    halfway = HEAD // 2
    exponent = jnp.arange(halfway, dtype=F32) * (2.0 / HEAD)
    frequency = jnp.exp(-math.log(10000.0) * exponent)
    angles = positions.astype(F32)[:, None] * frequency[None, :]
    cosine, sine = jnp.cos(angles), jnp.sin(angles)
    return jnp.concatenate([cosine, cosine], axis=-1), jnp.concatenate([-sine, sine], axis=-1)


def shifted(value, axis, size, shift):
    return lax.ppermute(value, axis, [(i, (i + shift) % size) for i in range(size)])


def swapped(value, axis, size):
    return lax.ppermute(value, axis, [(i, i ^ 1) for i in range(size)])


def dot(a, b, over=(1, 0)):
    return lax.dot_general(
        a, b, (((over[0],), (over[1],)), ((), ())), preferred_element_type=F32
    )


def at_distance(at_ref, distance):
    return lax.rem(at_ref[0] - distance + NX, NX)


def pick_kernel(at_ref, *refs):
    near, (mine_ref, theirs_ref, out_ref, sems) = refs[:NX], refs[NX:]
    core, reads = at_ref[1], out_ref.shape[1]
    for distance in range(NX):
        column = at_distance(at_ref, distance)
        for read in range(reads):
            block = near[distance][read // NEIGH, read % NEIGH]
            row, same = lax.rem(block // NC, NY), lax.rem(block, NC) == core
            sem = sems.at[distance * reads + read]

            @pl.when(same)
            def _():
                pltpu.make_async_copy(mine_ref.at[row], out_ref.at[column, read], sem).start()

            @pl.when(jnp.logical_not(same))
            def _():
                pltpu.make_async_copy(theirs_ref.at[row], out_ref.at[column, read], sem).start()

    for count in range(NX * reads):
        place = out_ref.at[count // reads, count % reads]
        pltpu.make_async_copy(mine_ref.at[0], place, sems.at[count]).wait()


def spread_kernel(ids_ref, from_ref, out_ref):
    reads = from_ref.shape[1]
    spans = reads // NEIGH
    for read in range(reads):
        owner = ids_ref[read // NEIGH, read % NEIGH]
        block = from_ref[owner // (NY * NC), read]
        for at in range(read // NEIGH, NZ, spans):
            out_ref[at, read % NEIGH] = block


def sum_kernel(from_ref, out_ref):
    spans = out_ref.shape[1] // NEIGH
    for read in range(out_ref.shape[1]):
        total = from_ref[read // NEIGH, read % NEIGH].astype(F32)
        for at in range(read // NEIGH + spans, NZ, spans):
            total = total + from_ref[at, read % NEIGH].astype(F32)
        for column in range(NX):
            out_ref[column, read] = total.astype(BF16)


def owner_kernel(at_ref, *refs):
    near, (from_ref, mine_ref, theirs_ref, total) = refs[:NX], refs[NX:]
    total[...] = jnp.zeros_like(total)
    here, core = at_ref[0], at_ref[1]
    for distance in range(NX):
        column = at_distance(at_ref, distance)
        for read in range(from_ref.shape[1]):
            block = near[distance][read // NEIGH, read % NEIGH]

            @pl.when(block // (NY * NC) == here)
            def _():
                side = jnp.where(lax.rem(block, NC) == core, 0, NY)
                at = side + lax.rem(block // NC, NY)
                total[at] = total[at] + from_ref[column, read].astype(F32)

    mine_ref[...] = total[:NY]
    theirs_ref[...] = total[NY:].astype(BF16)


def attention_kernel(
    tok, w_own, q_own, g_own, from_pair, kc, ks, qc, qs, w_far,
    part, dq_own, dq_pair, dk_all, dv_all, w_pair, sem,
):
    fetch = pltpu.make_async_copy(w_far, w_pair, sem)
    fetch.start()
    scale = 1.0 / math.sqrt(HEAD)
    half = HEAD // 2
    width = w_own.shape[2]
    rows = jnp.concatenate([tok[:, n].reshape(NLEN, DE) for n in range(NEIGH)], axis=0)
    projected = [(dot(rows, w_own[0]), dot(rows, w_own[1]).astype(BF16))]
    fetch.wait()
    projected.append((dot(rows, w_pair[0]), dot(rows, w_pair[1]).astype(BF16)))
    key_cos, key_sin, query_cos, query_sin = kc[...], ks[...], qc[...], qs[...]
    for turn, (q, g, dq) in enumerate((
        (q_own, g_own, dq_own),
        (from_pair.at[:SPAN], from_pair.at[SPAN:], dq_pair),
    )):
        key_raw, values = projected[turn]
        for head in range(width // HEAD):
            cols = slice(head * HEAD, (head + 1) * HEAD)
            place = slice(turn * width + head * HEAD, turn * width + (head + 1) * HEAD)
            raw = key_raw[:, cols]
            key = (raw * key_cos + pltpu.roll(raw, half, 1) * key_sin).astype(BF16)
            value = values[:, cols]
            wide = q[:, cols].astype(F32)
            query = (wide * query_cos + pltpu.roll(wide, half, 1) * query_sin).astype(BF16)
            grad = g[:, cols]
            exponentials = jnp.exp(dot(query, key, (1, 1)) * scale)
            weights = exponentials / jnp.sum(exponentials, axis=-1, keepdims=True)
            weights_low = weights.astype(BF16)
            grad_weights = dot(grad, value, (1, 1))
            delta = jnp.sum(weights_low.astype(F32) * grad_weights, axis=-1, keepdims=True)
            grad_scores = (weights * (grad_weights - delta) * scale).astype(BF16)
            dv_all[:, place] = dot(weights_low, grad, (0, 0)).astype(BF16)
            grad_query = dot(grad_scores, key)
            dq[:, cols] = (
                grad_query * query_cos - pltpu.roll(grad_query, half, 1) * query_sin
            ).astype(BF16)
            grad_key = dot(grad_scores, query, (0, 0))
            dk_all[:, place] = (
                grad_key * key_cos - pltpu.roll(grad_key, half, 1) * key_sin
            ).astype(BF16)
    product = dot(dk_all[:, :width], w_own[0], (1, 1)) + dot(dv_all[:, :width], w_own[1], (1, 1))
    product = product + dot(dk_all[:, width:], w_pair[0], (1, 1))
    product = product + dot(dv_all[:, width:], w_pair[1], (1, 1))
    for n in range(NEIGH):
        piece = product[n * NLEN:(n + 1) * NLEN].astype(BF16)
        part[:, n] = piece.reshape(NZ, ROWS, DE)


def on_core(kernel, name, shapes, scalars, *operands, scratch=(), space=VMEM):
    return pl.pallas_call(
        kernel,
        out_shape=shapes,
        in_specs=[SMEM] * len(scalars) + [space] * len(operands),
        out_specs=jax.tree.map(lambda _: space, shapes),
        scratch_shapes=scratch,
        compiler_params=pltpu.CompilerParams(vmem_limit_bytes=16 << 20),
        name=name,
    )(*scalars, *operands)


def attention(*operands):
    _, depth, width = operands[1].shape
    return pl.pallas_call(
        attention_kernel,
        out_shape=(
            jax.ShapeDtypeStruct((NZ, NEIGH, ROWS, DE), BF16),
            jax.ShapeDtypeStruct((SPAN, width), BF16),
            jax.ShapeDtypeStruct((SPAN, width), BF16),
        ),
        in_specs=[VMEM] * (len(operands) - 1) + [ANY],
        out_specs=(VMEM, VMEM, VMEM),
        scratch_shapes=[
            pltpu.VMEM((NEIGH * NLEN, 2 * width), BF16),
            pltpu.VMEM((NEIGH * NLEN, 2 * width), BF16),
            pltpu.VMEM((2, depth, width), BF16),
            pltpu.SemaphoreType.DMA,
        ],
        compiler_params=pltpu.CompilerParams(vmem_limit_bytes=40 << 20),
        cost_estimate=pl.CostEstimate(
            flops=2_100_000_000, bytes_accessed=6_000_000, transcendentals=131072
        ),
        name="attention",
    )(*operands)


def local(queries, out_grad, encodings, kv_weight, neighbour_ids, rot_offset):
    x_at, c_at, z_at = lax.axis_index("x"), lax.axis_index("c"), lax.axis_index("z")
    spans = neighbour_ids.shape[0]
    reads = spans * NEIGH
    span_at = z_at % 2

    w_far = swapped(kv_weight, "z", NZ)
    rows_q = queries.reshape(spans, SPAN, -1)
    rows_g = out_grad.reshape(spans, SPAN, -1)
    other = jnp.concatenate(
        [
            lax.dynamic_index_in_dim(rows_q, 1 - span_at, 0, keepdims=False),
            lax.dynamic_index_in_dim(rows_g, 1 - span_at, 0, keepdims=False),
        ],
        axis=0,
    )
    q_own = lax.dynamic_index_in_dim(rows_q, span_at, 0, keepdims=False)
    g_own = lax.dynamic_index_in_dim(rows_g, span_at, 0, keepdims=False)
    offsets = lax.dynamic_index_in_dim(rot_offset, span_at, 0, keepdims=False)
    positions = offsets[:, None] + jnp.arange(NLEN, dtype=jnp.int32)[None, :]
    key_cos, key_sin = rotary_tables(positions.reshape(NEIGH * NLEN))
    query_cos, query_sin = rotary_tables(jnp.arange(SPAN, dtype=jnp.int32))

    at = jnp.stack([x_at, c_at])
    near = [neighbour_ids] + [shifted(neighbour_ids, "x", NX, s) for s in range(1, NX)]
    copies = jnp.broadcast_to(encodings, (NY, ROWS, DE))
    over_y = lax.all_to_all(copies, "y", split_axis=0, concat_axis=0, tiled=True)
    over_y, near[:-1], other = lax.optimization_barrier((over_y, near[:-1], other))
    beside = swapped(over_y, "c", NC)
    block = (reads, ROWS, DE)
    asked = on_core(
        pick_kernel, "pick", jax.ShapeDtypeStruct((NX, *block), BF16), (at, *near),
        over_y, beside, scratch=[pltpu.SemaphoreType.DMA((NX * reads,))], space=ANY,
    )
    found = lax.all_to_all(asked, "x", split_axis=0, concat_axis=0, tiled=True)

    to_z = on_core(
        spread_kernel, "spread", jax.ShapeDtypeStruct((NZ, NEIGH, ROWS, DE), BF16), (neighbour_ids,),
        found,
    )
    from_pair = swapped(other, "z", NZ)
    to_z, w_far = lax.optimization_barrier((to_z, w_far))
    tok = lax.all_to_all(to_z, "z", split_axis=0, concat_axis=0, tiled=True)
    part, dq_own, dq_pair = attention(
        tok, kv_weight, q_own, g_own, from_pair,
        key_cos, key_sin, query_cos, query_sin, w_far,
    )

    from_heads = lax.all_to_all(part, "z", split_axis=0, concat_axis=0, tiled=True)
    read_copies = on_core(
        sum_kernel, "sums", jax.ShapeDtypeStruct((NX, *block), BF16), (), from_heads
    )
    read_copies, dq_pair = lax.optimization_barrier((read_copies, dq_pair))
    read_x = lax.all_to_all(read_copies, "x", split_axis=0, concat_axis=0, tiled=True)
    dq_back = swapped(dq_pair, "z", NZ)
    read_x, dq_back = lax.optimization_barrier((read_x, dq_back))
    first = jnp.where(span_at == 0, dq_own, dq_back)
    second = jnp.where(span_at == 0, dq_back, dq_own)
    grad_query = jnp.concatenate([first, second], axis=0)
    owners = (NY, ROWS, DE)
    mine, theirs = on_core(
        owner_kernel, "owner_sums",
        (jax.ShapeDtypeStruct(owners, F32), jax.ShapeDtypeStruct(owners, BF16)),
        (at, *near), read_x, scratch=[pltpu.VMEM((NC * NY, ROWS, DE), F32)],
    )
    owner_part = (mine + swapped(theirs, "c", NC).astype(F32)).astype(BF16)
    owner_part, grad_query = lax.optimization_barrier((owner_part, grad_query))
    from_y = lax.all_to_all(owner_part, "y", split_axis=0, concat_axis=0, tiled=True)
    owned = jnp.sum(from_y.astype(F32), axis=0)
    return (grad_query, owned.reshape(1, ROWS, DE))


def solution(mesh):
    fine = Mesh(mesh.devices.reshape(NX, NY, NC, NZ), ("x", "y", "c", "z"))
    enc = ("x", "y", "c")
    in_specs = (
        P(enc, "z"),
        P(enc, "z"),
        P(enc, "z", None),
        P(None, None, "z"),
        P(enc, None),
        P(enc, None),
    )
    out_specs = (P(enc, "z"), P(enc, "z", None))
    return jax.shard_map(local, mesh=fine, in_specs=in_specs, out_specs=out_specs, check_vma=False)
```
